32 devices in a mesh: items: 4 (over y, core), blk: 8 (over z, x).
Axes of the slice: x: 2, y: 2, z: 4, core: 2. Of those that a mesh axis runs over, the one named last changes fastest.
Arguments:
- decoder_in: bfloat16 [128, 128, 1024], P(('items', 'blk')), may hold values from -6 to 6
- memory: bfloat16 [128, 1024, 1024], P('items', 'blk'), may hold values from -6 to 6
- segment_ids: int32 [128, 128], P(('items', 'blk')), may hold values from 0 to 3, never falling along the last dimension, each value on 1 to 64 neighbouring positions
- memory_lengths: int32 [128], P(('items', 'blk')), may hold values from 51 to 1024
- w_self_in: bfloat16 [1024, 3072], P('blk'), may hold values from -0.1875 to 0.1875
- w_self_out: bfloat16 [1024, 1024], P('blk'), may hold values from -0.75 to 0.75
- w_cross_query: bfloat16 [1024, 1024], P('blk'), may hold values from -0.1875 to 0.1875
- w_cross_pair: bfloat16 [1024, 2048], P('blk'), may hold values from -0.1875 to 0.1875
- w_cross_out: bfloat16 [1024, 1024], P('blk'), may hold values from -3 to 3
- w_feed_up: bfloat16 [1024, 4096], P('blk'), may hold values from -0.1875 to 0.1875
- w_feed_down: bfloat16 [4096, 1024], P('blk'), may hold values from -0.09375 to 0.09375
- shifts: bfloat16 [10, 1024], P(None, 'blk'), may hold values from -2 to 2
- norm_gains: bfloat16 [3, 1024], P(None, 'blk'), may hold values from 0.5 to 1.5
- feed_bias: bfloat16 [4096], P('blk'), may hold values from -2 to 2
- out_grad: bfloat16 [128, 128, 1024], P(('items', 'blk')), may hold values from -6 to 6
Outputs:
- block_out: bfloat16 [128, 128, 1024], P(('items', 'blk'))
- decoder_grad: bfloat16 [128, 128, 1024], P(('items', 'blk'))
- memory_grad: bfloat16 [128, 1024, 1024], P('items', 'blk')
- grad_self_in: float32 [1024, 3072], P('blk')
- grad_self_out: float32 [1024, 1024], P('blk')
- grad_cross_query: float32 [1024, 1024], P('blk')
- grad_cross_pair: float32 [1024, 2048], P('blk')
- grad_cross_out: float32 [1024, 1024], P('blk')
- grad_feed_up: float32 [1024, 4096], P('blk')
- grad_feed_down: float32 [4096, 1024], P('blk')
- grad_shifts: float32 [10, 1024], P(None, 'blk')
- grad_norm_gains: float32 [3, 1024], P(None, 'blk')
- grad_feed_bias: float32 [4096], P('blk')
The draws below stay inside these ranges and needn't reach their ends.
Inputs may be any that keep to these rules, and one draw needn't show every extreme that they name: `segment_ids`: ids never fall along an item's positions.
All inputs are finite; a program needn't handle non-finite values.
Results may differ from the reference program's by a relative error of at most 0.023.
Values may be sent and summed in bfloat16 or wider, within the bound.
No kernel may reach another device: no remote copies, remote signals or barrier semaphores. Data moves between devices by JAX's collectives and lax.ppermute only.
A program may use at most 256 MiB of HBM per device.

```python
import math
import jax
import jax.numpy as jnp
import numpy as np
from jax import lax

D = 1024
HEADS = 16
FF = 4096
DEC = 128
MEM = 1024
GROUP = 32
ITEMS = 128


def draw_memory_lengths(key, part):
    key = jax.random.fold_in(key, 7)
    short_key, pick_key = jax.random.split(key)
    drawn = jax.random.randint(short_key, (ITEMS,), MEM // 20, MEM + 1)
    chosen = jax.random.randint(pick_key, (ITEMS // GROUP,), 0, GROUP)
    offsets = jnp.arange(ITEMS) % GROUP
    chosen_rows = jnp.repeat(chosen, GROUP)
    return jnp.where(offsets == chosen_rows, MEM, drawn).astype(jnp.int32)


def strengthened(entries, key, source, target, shards_of, factor):
    def block_of(dim):
        return (jnp.arange(entries.shape[dim]) // (entries.shape[dim] // shards_of)).reshape((-1,) + (1,) * (entries.ndim - 1 - dim))

    first = jax.random.permutation(key, shards_of)[block_of(target)]
    second = (block_of(target) + shards_of // 2) % shards_of
    return jnp.where((block_of(source) == first) | (block_of(source) == second), factor * entries, entries)


def levels(stream_key, shape, cuts, smallest, high):
    loudness = 1.0
    for dim, blocks in cuts:
        heights = jax.random.uniform(jax.random.fold_in(jax.random.fold_in(stream_key, 6), dim), (blocks,), jnp.float32, smallest / len(cuts), high / len(cuts))
        loudness = loudness * jnp.repeat(jnp.exp(heights), shape[dim] // blocks).reshape((-1,) + (1,) * (len(shape) - 1 - dim))
    return loudness


def split_up(number_of, total, most, skew):
    weights = [(1 << 20) // math.isqrt(standing ** skew) + 1 for standing in range(2, number_of + 1)]
    rest, holding = total - most - (number_of - 1), [1] * (number_of - 1)
    while rest > 0:
        movable = [i for i in range(number_of - 1) if holding[i] < most]
        whole, left = sum([weights[i] for i in movable]), rest
        for i in movable:
            extra = min(most - holding[i], max(1, left * weights[i] // whole), rest)
            holding[i] = holding[i] + extra
            rest = rest - extra
    return np.array([most] + holding)


def uneven(rng, count, total, limit, lean):
    if count == 2:
        one = jax.random.randint(rng, (), max(1, total - limit), min(limit, total - 1) + 1)
        return jnp.stack([one, total - one])
    tallies = jnp.asarray(split_up(count, total, limit, lean), jnp.int32)
    pairs = (count - 1) // 2
    giver, sink = tallies[1:1 + 2 * pairs:2], tallies[2:2 + 2 * pairs:2]
    slack = jnp.minimum(giver - 1, limit - sink)
    moved = jax.random.randint(jax.random.fold_in(rng, 1), (pairs,), 0, 1 << 20) % (slack + 1)
    tallies = tallies.at[1:1 + 2 * pairs:2].set(giver - moved).at[2:2 + 2 * pairs:2].set(sink + moved)
    return tallies[jax.random.permutation(jax.random.fold_in(rng, 2), count)]


def bell_draw(key, dims, width, limit, shards=(), held_as=jnp.bfloat16):
    values = width * jax.random.normal(key, dims, jnp.float32)
    if shards:
        values = values * levels(key, dims, shards, -0.22, 0.18)
    return jnp.clip(values, -limit, limit).astype(held_as)


def gaussian_with(key, extent, scale, bound, pieces, heavy, dtype=jnp.bfloat16):
    values = scale * jax.random.normal(key, extent, jnp.float32)
    if pieces:
        values = values * levels(key, extent, pieces, -0.22, 0.18)
    return jnp.clip(strengthened(values, jax.random.fold_in(key, 3), *heavy), -bound, bound).astype(dtype)


def setup_inputs(seed: int = 0) -> dict:
    streams_of = jax.random.split(jax.random.key(seed), 16)
    decoder_in = bell_draw(streams_of[0], (ITEMS, DEC, D), 1.0, 6.0, ((0, 32),))
    memory = bell_draw(streams_of[1], (ITEMS, MEM, D), 1.0, 6.0, ((0, 4), (1, 8)))
    segment_ids = jax.vmap(lambda own: jnp.searchsorted(jnp.cumsum(uneven(own, 4, DEC, DEC // 2, 0)), jnp.arange(DEC), side="right"))(jax.random.split(streams_of[2], ITEMS)).reshape((ITEMS, DEC)).astype(jnp.int32)
    memory_lengths = draw_memory_lengths(jax.random.fold_in(streams_of[15], 71), 0)
    w_self_in = bell_draw(streams_of[4], (D, 3 * D), D ** -0.5, 0.1875, ((0, 8),))
    w_self_out = bell_draw(streams_of[5], (D, D), (D // 16) ** -0.5, 0.75, ((0, 8),))
    w_cross_query = bell_draw(streams_of[6], (D, D), D ** -0.5, 0.1875, ((0, 8),))
    w_cross_pair = bell_draw(streams_of[7], (D, 2 * D), D ** -0.5, 0.1875, ((0, 8),))
    w_cross_out = bell_draw(streams_of[8], (D, D), (max(2, D // 256)) ** -0.5, 3.0, ((0, 8),))
    w_feed_up = bell_draw(streams_of[9], (D, FF), D ** -0.5, 0.1875, ((0, 8),))
    w_feed_down = bell_draw(streams_of[10], (FF, D), FF ** -0.5, 0.09375, ((0, 8),))
    shifts = bell_draw(streams_of[11], (10, D), 0.3, 2.0, ((1, 8),))
    norm_gains = jnp.clip(1.0 + 0.1 * jax.random.normal(streams_of[12], (3, D), jnp.float32), 0.5, 1.5).astype(jnp.bfloat16)
    feed_bias = bell_draw(streams_of[13], (FF,), 0.3, 2.0, ((0, 8),))
    out_grad = gaussian_with(streams_of[14], (ITEMS, DEC, D), 1.0, 6.0, ((0, 32),), (0, 2, 32, 2.75))
    return dict(decoder_in=decoder_in, memory=memory, segment_ids=segment_ids, memory_lengths=memory_lengths, w_self_in=w_self_in, w_self_out=w_self_out, w_cross_query=w_cross_query, w_cross_pair=w_cross_pair, w_cross_out=w_cross_out, w_feed_up=w_feed_up, w_feed_down=w_feed_down, shifts=shifts, norm_gains=norm_gains, feed_bias=feed_bias, out_grad=out_grad)


precise = lax.Precision.HIGHEST

@jax.custom_vjp
def low(v):
    return lax.optimization_barrier(v.astype(jnp.bfloat16)).astype(jnp.float32)

@jax.custom_vjp
def low_back(v):
    return v

def low_keep(v):
    return (low(v), None)

def low_pass(kept, grad):
    return (grad,)

def back_keep(v):
    return (v, None)

def back_low(kept, grad):
    return (low(grad),)
low.defvjp(low_keep, low_pass)
low_back.defvjp(back_keep, back_low)

def both_ways(value):
    return low_back(low(value))

def matmul(left, right):
    return jnp.dot(left, right, precision=precise, preferred_element_type=jnp.float32)

def layer_norm(values, gain, shift):
    centre = values - lax.optimization_barrier(jnp.mean(values, axis=-1, keepdims=True))
    spread = lax.optimization_barrier(jnp.mean(centre * centre, axis=-1, keepdims=True))
    return centre * lax.rsqrt(spread + 1e-05) * gain + shift

def attend(queries, key_rows, value_rows, allowed):
    scores = low_back(jnp.einsum('bqhd,bkhd->bhqk', queries, key_rows, precision=precise))
    scores = jnp.where(allowed[:, None], scores, -1e+30)
    largest = lax.optimization_barrier(jnp.max(scores, axis=-1, keepdims=True))
    weights = jnp.exp(scores - largest)
    probability = weights / lax.optimization_barrier(jnp.sum(weights, axis=-1, keepdims=True))
    return jnp.einsum('bhqk,bkhd->bqhd', low(probability), value_rows, precision=precise)

def decoder_block(params, decoder_in, memory, segment_ids, memory_lengths):
    w_self_in, w_self_out, w_cross_query, w_cross_pair, w_cross_out, w_feed_up, w_feed_down, shifts, norm_gains, feed_bias = params
    block_items = decoder_in.shape[0]
    head_size = D // HEADS
    query_scale = head_size ** (-0.5)
    token_rows = decoder_in.reshape(block_items * DEC, D)
    head_shape = (block_items, DEC, HEADS, head_size)
    projected = matmul(token_rows, w_self_in)
    queries = both_ways((projected[:, :D] + shifts[0]) * query_scale)
    key_rows = both_ways(projected[:, D:2 * D])
    value_rows = both_ways(projected[:, 2 * D:] + shifts[1])
    position = jnp.arange(DEC)
    causal = position[None, :] <= position[:, None]
    self_allowed = (segment_ids[:, :, None] == segment_ids[:, None, :]) & causal[None]
    attended = attend(queries.reshape(head_shape), key_rows.reshape(head_shape), value_rows.reshape(head_shape), self_allowed)
    attended = both_ways(attended.reshape(block_items * DEC, D))
    branch = low_back(matmul(attended, w_self_out) + shifts[2])
    hidden = layer_norm(token_rows + branch, norm_gains[0], shifts[7])
    cross_queries = both_ways((matmul(low(hidden), w_cross_query) + shifts[3]) * query_scale)
    memory_rows = memory.reshape(block_items * MEM, D)
    pair_rows = matmul(memory_rows, w_cross_pair)
    memory_head = (block_items, MEM, HEADS, head_size)
    memory_keys = both_ways(pair_rows[:, :D]).reshape(memory_head)
    memory_values = both_ways(pair_rows[:, D:] + shifts[4]).reshape(memory_head)
    slot_index = jnp.arange(MEM)
    live = slot_index[None, :] < memory_lengths[:, None]
    memory_allowed = jnp.broadcast_to(live[:, None, :], (block_items, DEC, MEM))
    cross_attended = attend(cross_queries.reshape(head_shape), memory_keys, memory_values, memory_allowed)
    cross_attended = both_ways(cross_attended.reshape(block_items * DEC, D))
    cross_branch = low_back(matmul(cross_attended, w_cross_out) + shifts[5])
    second = layer_norm(hidden + cross_branch, norm_gains[1], shifts[8])
    upward = low_back(matmul(low(second), w_feed_up) + feed_bias)
    activation = low(jax.nn.gelu(upward, approximate=False))
    feed_branch = low_back(matmul(activation, w_feed_down) + shifts[6])
    result = layer_norm(second + feed_branch, norm_gains[2], shifts[9])
    return result.reshape(block_items, DEC, D)

def reference(decoder_in, memory, segment_ids, memory_lengths, w_self_in, w_self_out, w_cross_query, w_cross_pair, w_cross_out, w_feed_up, w_feed_down, shifts, norm_gains, feed_bias, out_grad):
    params = tuple((entry.astype(jnp.float32) for entry in (w_self_in, w_self_out, w_cross_query, w_cross_pair, w_cross_out, w_feed_up, w_feed_down, shifts, norm_gains, feed_bias)))
    per_block = math.gcd(ITEMS, max(1, 4096 // DEC))
    blocks = ITEMS // per_block

    def regroup(array):
        return array.reshape((blocks, per_block) + array.shape[1:])
    segments = regroup(segment_ids)
    lengths = regroup(memory_lengths)

    def forward(inputs, memory_inputs, weights_all):

        def one_block(carried):
            return decoder_block(weights_all, carried[0], carried[1], carried[2], carried[3])
        outputs = lax.map(jax.checkpoint(one_block), (regroup(inputs), regroup(memory_inputs), segments, lengths))
        return outputs.reshape(inputs.shape)
    block_out, pullback = jax.vjp(forward, decoder_in.astype(jnp.float32), memory.astype(jnp.float32), params)
    decoder_grad, memory_grad, param_grads = pullback(out_grad.astype(jnp.float32))
    return (block_out.astype(jnp.bfloat16), decoder_grad.astype(jnp.bfloat16), memory_grad.astype(jnp.bfloat16), param_grads[0], param_grads[1], param_grads[2], param_grads[3], param_grads[4], param_grads[5], param_grads[6], param_grads[7], param_grads[8], param_grads[9])
```

```python
import jax
import jax.numpy as jnp
from jax import lax
from jax.experimental import pallas as pl
from jax.experimental.pallas import tpu as pltpu
from jax.sharding import PartitionSpec as P

HEADS = 16
CHUNKS = 8
BF = jnp.bfloat16
F32 = jnp.float32
VMEM_BYTES = 56 * 1024 * 1024


def move(axis, pairs):
    return lambda value: lax.ppermute(value, axis, pairs)


swap_x = move("blk", [(i, i ^ 1) for i in range(8)])
go_up = move("blk", [(i, (i + 2) % 8) for i in range(8)])
go_down = move("blk", [((i + 2) % 8, i) for i in range(8)])
go_up_x = move("blk", [(i, ((i + 2) % 8) ^ 1) for i in range(8)])
go_down_x = move("blk", [((i + 2) % 8, i ^ 1) for i in range(8)])
swap_core = move("items", [(i, i ^ 1) for i in range(4)])
swap_y = move("items", [(i, i ^ 2) for i in range(4)])


def places():
    me = lax.axis_index("blk")
    return [((me + 2 * (k // 2)) % 8) ^ (k % 2) for k in range(8)]


def collect(own, flip):
    ahead, behind = (go_down, go_up) if flip else (go_up, go_down)
    dz_a, dz_b = (1, 3) if flip else (3, 1)
    across = swap_x(own)
    a, b = ahead(own), behind(own)
    ax, bx = ahead(across), behind(across)
    far = ahead(a)
    far_x = swap_x(far)
    found = {1: across, 2 * dz_a: a, 2 * dz_b: b, 2 * dz_a + 1: ax, 2 * dz_b + 1: bx}
    found.update({4: far, 5: far_x})
    return [found[k] for k in range(1, 8)]


def place_kernel(widths, *refs):
    spots, own, mine, other = refs[0], refs[1], refs[2:9], refs[9:16]
    outs, held, in_sem, out_sem = refs[16:-3], refs[-3], refs[-2], refs[-1]
    rows = own.shape[0]
    half = rows // 2
    core = spots[8]
    arriving, rows_of = [], []
    for k in range(8):
        base = spots[k] * rows
        parts = [(own, base, rows)] if k == 0 else [
            (mine[k - 1], base + core * half, half),
            (other[k - 1], base + (1 - core) * half, half),
        ]
        for source, row, count in parts:
            span = pl.ds(pl.multiple_of(row, 16), count)
            copy = pltpu.make_async_copy(source, held.at[span, :], in_sem.at[len(arriving)])
            copy.start()
            arriving.append(copy)
            rows_of.append(span)
    leaving = []
    for copy, span in zip(arriving, rows_of):
        copy.wait()
        column = 0
        for out, width in zip(outs, widths):
            onward = pltpu.make_async_copy(
                held.at[span, pl.ds(column, width)], out.at[span, :], out_sem.at[len(leaving)]
            )
            onward.start()
            leaving.append(onward)
            column += width
    for copy in leaving:
        copy.wait()


def spot_vector():
    return jnp.stack(places() + [lax.axis_index("items") % 2]).astype(jnp.int32)


def gather_rows(shards, flip):
    own = shards[0] if len(shards) == 1 else jnp.concatenate(shards, axis=1)
    rows, columns = own.shape
    widths = [s.shape[1] for s in shards]
    core = lax.axis_index("items") % 2
    mine = collect(lax.dynamic_slice_in_dim(own, core * (rows // 2), rows // 2, 0), flip)
    other = [swap_core(piece) for piece in mine]
    any_spec = pl.BlockSpec(memory_space=pl.ANY)
    return pl.pallas_call(
        lambda *refs: place_kernel(widths, *refs),
        out_shape=[jax.ShapeDtypeStruct((8 * rows, w), own.dtype) for w in widths],
        in_specs=[pl.BlockSpec(memory_space=pltpu.SMEM)] + [any_spec] * 15,
        out_specs=[any_spec] * len(widths),
        scratch_shapes=[
            pltpu.VMEM((8 * rows, columns), own.dtype),
            pltpu.SemaphoreType.DMA((15,)),
            pltpu.SemaphoreType.DMA((15 * len(widths),)),
        ],
        compiler_params=pltpu.CompilerParams(vmem_limit_bytes=VMEM_BYTES),
        cost_estimate=pl.CostEstimate(
            flops=0, bytes_accessed=32 * rows * columns, transcendentals=0
        ),
        name="place_rows",
    )(spot_vector(), own, *mine, *other)


def add_low(*terms):
    total = terms[0].astype(F32)
    for term in terms[1:]:
        total = total + term.astype(F32)
    return total.astype(BF)


def reduce_rows(full, flip):
    rows = full.shape[0] // 8
    half = rows // 2
    columns = full.shape[1]
    core = lax.axis_index("items") % 2
    halves = full.reshape(8, 2, half, columns)
    kept = lax.dynamic_slice_in_dim(halves, core, 1, 1)[:, 0]
    sent = lax.dynamic_slice_in_dim(halves, 1 - core, 1, 1)[:, 0]
    both = add_low(kept, swap_core(sent))
    part = [lax.dynamic_index_in_dim(both, j, 0, keepdims=False) for j in places()]
    ahead, behind = (go_down, go_up) if flip else (go_up, go_down)
    dz_a, dz_b = (1, 3) if flip else (3, 1)
    far = add_low(part[4], swap_x(part[5]))
    near = add_low(part[2 * dz_a], behind(far))
    across = add_low(part[1], behind(part[2 * dz_a + 1]), ahead(part[2 * dz_b + 1]))
    done = add_low(part[0], swap_x(across), behind(near), ahead(part[2 * dz_b]))
    done = add_low(done, swap_y(done))
    partner = swap_core(done)
    first = jnp.where(core == 0, done, partner)
    second = jnp.where(core == 0, partner, done)
    return jnp.concatenate([first, second], axis=0).astype(F32)


def exchange(blocks):
    return [
        blocks[0],
        swap_x(blocks[1]),
        go_down(blocks[6]),
        go_down_x(blocks[7]),
        go_up(go_up(blocks[4])),
        go_down_x(go_down(blocks[5])),
        go_up(blocks[2]),
        go_up_x(blocks[3]),
    ]


def join_kernel(*refs):
    spots, blocks, out, held, in_sem, out_sem = refs[0], refs[1:9], *refs[9:]
    count = blocks[0].shape[0]
    arriving = [
        pltpu.make_async_copy(blocks[k], held.at[k], in_sem.at[k]) for k in range(8)
    ]
    leaving = [
        pltpu.make_async_copy(
            held.at[k], out.at[pl.ds(spots[k] * count, count)], out_sem.at[k]
        )
        for k in range(8)
    ]
    for copy in arriving:
        copy.start()
    for copy, onward in zip(arriving, leaving):
        copy.wait()
        onward.start()
    for copy in leaving:
        copy.wait()


def join_items(blocks):
    any_spec = pl.BlockSpec(memory_space=pl.ANY)
    shape = blocks[0].shape
    return pl.pallas_call(
        join_kernel,
        out_shape=jax.ShapeDtypeStruct((8 * shape[0],) + shape[1:], blocks[0].dtype),
        in_specs=[pl.BlockSpec(memory_space=pltpu.SMEM)] + [any_spec] * 8,
        out_specs=any_spec,
        scratch_shapes=[
            pltpu.VMEM((8,) + shape, blocks[0].dtype),
            pltpu.SemaphoreType.DMA((8,)),
            pltpu.SemaphoreType.DMA((8,)),
        ],
        compiler_params=pltpu.CompilerParams(vmem_limit_bytes=VMEM_BYTES),
        name="join_items",
    )(spot_vector(), *blocks)


def dot_nt(left, right):
    return lax.dot_general(left, right, (((1,), (1,)), ((), ())), preferred_element_type=F32)


def dot_tn(left, right):
    return lax.dot_general(left, right, (((0,), (0,)), ((), ())), preferred_element_type=F32)


def dot_nn(left, right):
    return lax.dot_general(left, right, (((1,), (0,)), ((), ())), preferred_element_type=F32)


def two_heads(value):
    lane = lax.broadcasted_iota(jnp.int32, value.shape, 1)
    zero = jnp.zeros_like(value)
    return jnp.concatenate(
        [jnp.where(lane < 64, value, zero), jnp.where(lane < 64, zero, value)], axis=0
    )


def one_pair(turned):
    count = turned.shape[1] // 2
    joined = jnp.concatenate([turned[:64, :count], turned[64:, count:]], axis=0)
    return joined.T


def pair_forward(query, keys, values, masks):
    stacked = two_heads(query)
    scores = [mask(dot_nt(k, stacked)) for k, mask in zip(keys, masks)]
    top = scores[0].max(axis=0, keepdims=True)
    for s in scores[1:]:
        top = jnp.maximum(top, s.max(axis=0, keepdims=True))
    total, turned = None, None
    for s, v in zip(scores, values):
        weight = jnp.exp(s - top)
        add = weight.sum(axis=0, keepdims=True)
        product = dot_tn(v, weight.astype(BF))
        total = add if total is None else total + add
        turned = product if turned is None else turned + product
    return one_pair(turned * (1.0 / total)).astype(BF), top + jnp.log(total)


def pair_backward(query, incoming, keys, values, masks, log_total):
    stacked, grads = two_heads(query), two_heads(incoming)
    weights, changes, centre = [], [], None
    for k, v, mask in zip(keys, values, masks):
        weight = jnp.exp(mask(dot_nt(k, stacked)) - log_total)
        change = dot_nt(v, grads)
        add = (weight * change).sum(axis=0, keepdims=True)
        centre = add if centre is None else centre + add
        weights.append(weight)
        changes.append(change)
    key_grads, value_grads, turned = [], [], None
    for k, weight, change in zip(keys, weights, changes):
        score_grad = (weight * (change - centre)).astype(BF)
        key_grads.append(dot_nn(score_grad, stacked).astype(BF))
        value_grads.append(dot_nn(weight.astype(BF), grads).astype(BF))
        product = dot_tn(k, score_grad)
        turned = product if turned is None else turned + product
    return one_pair(turned).astype(BF), key_grads, value_grads


def slot_masks(starts, length, rows, columns):
    slot = lax.broadcasted_iota(jnp.int32, (rows, columns), 0)
    return [
        (lambda s, c=c: jnp.where(slot < length - starts[c], s, -1e30)) for c in range(CHUNKS)
    ]


PAIRS = 2


def cross_forward_kernel(lengths, starts, q_ref, kv_ref, out_ref, log_ref):
    rows = kv_ref.shape[2]
    masks = slot_masks(starts, lengths[pl.program_id(0)], rows, 2 * q_ref.shape[1])
    for p in range(PAIRS):
        keys = [kv_ref[c, 0, :, 256 * p : 256 * p + 128] for c in range(CHUNKS)]
        values = [kv_ref[c, 0, :, 256 * p + 128 : 256 * p + 256] for c in range(CHUNKS)]
        out, log_total = pair_forward(q_ref[0, :, 128 * p : 128 * p + 128], keys, values, masks)
        out_ref[0, :, 128 * p : 128 * p + 128] = out
        log_ref[0, p] = log_total


def cross_backward_kernel(
    lengths, starts, q_ref, grad_ref, kv_ref, log_ref, dq_ref, dkv_ref
):
    rows = kv_ref.shape[2]
    masks = slot_masks(starts, lengths[pl.program_id(0)], rows, 2 * q_ref.shape[1])
    for p in range(PAIRS):
        span = slice(128 * p, 128 * p + 128)
        keys = [kv_ref[c, 0, :, 256 * p : 256 * p + 128] for c in range(CHUNKS)]
        values = [kv_ref[c, 0, :, 256 * p + 128 : 256 * p + 256] for c in range(CHUNKS)]
        dq, dks, dvs = pair_backward(
            q_ref[0, :, span], grad_ref[0, :, span], keys, values, masks, log_ref[0, p]
        )
        dq_ref[0, :, span] = dq
        for c in range(CHUNKS):
            dkv_ref[c, 0, :, 256 * p : 256 * p + 128] = dks[c]
            dkv_ref[c, 0, :, 256 * p + 128 : 256 * p + 256] = dvs[c]


def cross_specs(items, length, width, rows):
    pairs = width // 128
    small = pl.BlockSpec((1, length, 128 * PAIRS), lambda i, p, *_: (i, 0, p))
    big = pl.BlockSpec((CHUNKS, 1, rows, 256 * PAIRS), lambda i, p, *_: (0, i, 0, p))
    logs = pl.BlockSpec((1, PAIRS, 1, 2 * length), lambda i, p, *_: (i, p, 0, 0))
    return (items, pairs // PAIRS), small, big, logs


def cross_forward(lengths, starts, queries, kv):
    items, length, width = queries.shape
    rows = kv.shape[2]
    grid, small, big, logs = cross_specs(items, length, width, rows)
    return pl.pallas_call(
        cross_forward_kernel,
        out_shape=[
            jax.ShapeDtypeStruct(queries.shape, BF),
            jax.ShapeDtypeStruct((items, width // 128, 1, 2 * length), F32),
        ],
        grid_spec=pltpu.PrefetchScalarGridSpec(
            num_scalar_prefetch=2, grid=grid, in_specs=[small, big], out_specs=[small, logs]
        ),
        compiler_params=pltpu.CompilerParams(vmem_limit_bytes=VMEM_BYTES),
        cost_estimate=pl.CostEstimate(
            flops=8 * items * length * CHUNKS * rows * width,
            bytes_accessed=2 * kv.size,
            transcendentals=items * length * CHUNKS * rows * HEADS,
        ),
        name="cross_forward",
    )(lengths, starts, queries, kv)


def cross_backward(lengths, starts, queries, grads, kv, logs_in):
    items, length, width = queries.shape
    rows = kv.shape[2]
    grid, small, big, logs = cross_specs(items, length, width, rows)
    return pl.pallas_call(
        cross_backward_kernel,
        out_shape=[jax.ShapeDtypeStruct(queries.shape, BF), jax.ShapeDtypeStruct(kv.shape, BF)],
        grid_spec=pltpu.PrefetchScalarGridSpec(
            num_scalar_prefetch=2,
            grid=grid,
            in_specs=[small, small, big, logs],
            out_specs=[small, big],
        ),
        compiler_params=pltpu.CompilerParams(vmem_limit_bytes=VMEM_BYTES),
        cost_estimate=pl.CostEstimate(
            flops=20 * items * length * CHUNKS * rows * width,
            bytes_accessed=4 * kv.size,
            transcendentals=items * length * CHUNKS * rows * HEADS,
        ),
        name="cross_backward",
    )(lengths, starts, queries, grads, kv, logs_in)


def self_mask(seg_row, seg_column, length):
    key = lax.broadcasted_iota(jnp.int32, (length, length), 0)
    query = lax.broadcasted_iota(jnp.int32, (length, length), 1)
    allowed = jnp.where((seg_column == seg_row) & (key <= query), 1.0, 0.0)
    allowed = jnp.concatenate([allowed, allowed], axis=1)
    return lambda s: jnp.where(allowed > 0.5, s, -1e30)


def self_forward_kernel(seg_row, seg_column, qkv_ref, out_ref, log_ref):
    length, width = out_ref.shape[1:]
    mask = self_mask(seg_row[0], seg_column[0], length)
    for p in range(width // 128):
        span = slice(128 * p, 128 * p + 128)
        query = qkv_ref[0, :, span]
        key = qkv_ref[0, :, width + 128 * p : width + 128 * p + 128]
        value = qkv_ref[0, :, 2 * width + 128 * p : 2 * width + 128 * p + 128]
        out, log_total = pair_forward(query, [key], [value], [mask])
        out_ref[0, :, span] = out
        log_ref[0, p] = log_total


def self_backward_kernel(seg_row, seg_column, qkv_ref, grad_ref, log_ref, out_ref):
    length, width = grad_ref.shape[1:]
    mask = self_mask(seg_row[0], seg_column[0], length)
    for p in range(width // 128):
        span = slice(128 * p, 128 * p + 128)
        key_span = slice(width + 128 * p, width + 128 * p + 128)
        value_span = slice(2 * width + 128 * p, 2 * width + 128 * p + 128)
        dq, dk, dv = pair_backward(
            qkv_ref[0, :, span],
            grad_ref[0, :, span],
            [qkv_ref[0, :, key_span]],
            [qkv_ref[0, :, value_span]],
            [mask],
            log_ref[0, p],
        )
        out_ref[0, :, span] = dq * BF(0.125)
        out_ref[0, :, key_span] = dk[0]
        out_ref[0, :, value_span] = dv[0]


def self_specs(items, length, width):
    rows = pl.BlockSpec((1, 1, length), lambda i: (i, 0, 0))
    columns = pl.BlockSpec((1, length, 1), lambda i: (i, 0, 0))
    wide = pl.BlockSpec((1, length, 3 * width), lambda i: (i, 0, 0))
    slim = pl.BlockSpec((1, length, width), lambda i: (i, 0, 0))
    logs = pl.BlockSpec((1, width // 128, 1, 2 * length), lambda i: (i, 0, 0, 0))
    return rows, columns, wide, slim, logs


def self_forward(segments, qkv):
    items, length, width = qkv.shape[0], qkv.shape[1], qkv.shape[2] // 3
    rows, columns, wide, slim, logs = self_specs(items, length, width)
    return pl.pallas_call(
        self_forward_kernel,
        grid=(items,),
        out_shape=[
            jax.ShapeDtypeStruct((items, length, width), BF),
            jax.ShapeDtypeStruct((items, width // 128, 1, 2 * length), F32),
        ],
        in_specs=[rows, columns, wide],
        out_specs=[slim, logs],
        compiler_params=pltpu.CompilerParams(vmem_limit_bytes=VMEM_BYTES),
        name="self_forward",
    )(segments[:, None, :], segments[:, :, None], qkv)


def self_backward(segments, qkv, grads, logs_in):
    items, length, width = grads.shape
    rows, columns, wide, slim, logs = self_specs(items, length, width)
    return pl.pallas_call(
        self_backward_kernel,
        grid=(items,),
        out_shape=jax.ShapeDtypeStruct(qkv.shape, BF),
        in_specs=[rows, columns, wide, slim, logs],
        out_specs=wide,
        compiler_params=pltpu.CompilerParams(vmem_limit_bytes=VMEM_BYTES),
        name="self_backward",
    )(segments[:, None, :], segments[:, :, None], qkv, grads, logs_in)


def layer_norm(values, gain, shift):
    centre = values - jnp.mean(values, axis=-1, keepdims=True)
    spread = jnp.mean(centre * centre, axis=-1, keepdims=True)
    return centre * lax.rsqrt(spread + 1e-05) * gain + shift


def exact_gelu(values):
    return jax.nn.gelu(values, approximate=False)


def column_sum(values):
    return jnp.sum(values.astype(F32), axis=0)


def interleave(matrix):
    rows, columns = matrix.shape
    return matrix.reshape(rows, 2, columns // 256, 128).swapaxes(1, 2).reshape(rows, columns)


def part_again(matrix):
    rows, columns = matrix.shape
    return matrix.reshape(rows, columns // 256, 2, 128).swapaxes(1, 2).reshape(rows, columns)


def pack_small(shifts, gains, bias):
    width = shifts.shape[1]
    rows = jnp.concatenate([shifts, gains, bias.reshape(-1, width)], axis=0)
    return jnp.pad(rows, ((0, 32 - rows.shape[0]), (0, 0)))


def unpack_small(rows, width):
    count = rows.shape[0] // 32
    rows = rows.reshape(count, 32, width)
    shifts = rows[:, :10].transpose(1, 0, 2).reshape(10, -1)
    gains = rows[:, 10:13].transpose(1, 0, 2).reshape(3, -1)
    return shifts, gains, rows[:, 13:17].reshape(-1)


def per_device(tuned):
    def run(
        decoder_in,
        memory,
        segment_ids,
        memory_lengths,
        w_self_in,
        w_self_out,
        w_cross_query,
        w_cross_pair,
        w_cross_out,
        w_feed_up,
        w_feed_down,
        shifts,
        norm_gains,
        feed_bias,
        out_grad,
    ):
        item_count, length, width = decoder_in.shape
        row_count = item_count * length
        pair_shard = interleave(w_cross_pair)
        if tuned:
            small = pack_small(shifts, norm_gains, feed_bias)
            (small,) = gather_rows([small], False)
            shift_low, gain_low, feed_shift_low = unpack_small(small, shifts.shape[1])
            (self_proj,) = gather_rows([w_self_in], False)
            self_out, cross_query, cross_pair = gather_rows(
                [w_self_out, w_cross_query, pair_shard], True
            )
            spots = places()
            blocks = [lax.dynamic_slice_in_dim(memory, j * item_count, item_count, 0) for j in spots]
            arrived = exchange(blocks)
            starts = jnp.stack(spots).astype(jnp.int32) * memory.shape[1]
            cross_out, feed_up = gather_rows([w_cross_out, w_feed_up], False)
            (feed_down,) = gather_rows([w_feed_down], True)
            memory_rows = jnp.stack(arrived)
        else:
            def whole(shard, axis=0):
                return lax.all_gather(shard, "blk", axis=axis, tiled=True)

            shift_low, gain_low = whole(shifts, 1), whole(norm_gains, 1)
            feed_shift_low = whole(feed_bias)
            self_proj, self_out, cross_query = whole(w_self_in), whole(w_self_out), whole(w_cross_query)
            cross_pair, cross_out = whole(pair_shard), whole(w_cross_out)
            feed_up, feed_down = whole(w_feed_up), whole(w_feed_down)
            arrived = lax.all_to_all(memory, "blk", split_axis=0, concat_axis=1, tiled=True)
            slots = arrived.shape[1] // CHUNKS
            memory_rows = arrived.reshape(item_count, CHUNKS, slots, width).swapaxes(0, 1)
            starts = jnp.arange(CHUNKS, dtype=jnp.int32) * slots
        shift_rows = shift_low.astype(F32)
        gain_rows = gain_low.astype(F32)
        feed_shift = feed_shift_low.astype(F32)
        query_scale = (width // HEADS) ** (-0.5)
        three = (item_count, length, width)

        token_rows = decoder_in.reshape(row_count, width)
        no_shift = jnp.zeros((width,), F32)
        in_shift = jnp.concatenate([shift_rows[0], no_shift, shift_rows[1]])
        in_scale = jnp.concatenate([no_shift + query_scale, no_shift + 1.0, no_shift + 1.0])
        qkv = (
            (jnp.dot(token_rows, self_proj, preferred_element_type=F32) + in_shift) * in_scale
        ).astype(BF).reshape(item_count, length, 3 * width)
        attended, self_logs = self_forward(segment_ids, qkv)
        attended = attended.reshape(row_count, width)
        branch = jnp.dot(attended, self_out, preferred_element_type=F32) + shift_rows[2]
        hidden, first_norm_back = jax.vjp(
            layer_norm, token_rows.astype(F32) + branch, gain_rows[0], shift_rows[7]
        )
        hidden_low = hidden.astype(BF)

        cross_queries = (
            (jnp.dot(hidden_low, cross_query, preferred_element_type=F32) + shift_rows[3])
            * query_scale
        ).astype(BF).reshape(three)
        pair_shift = interleave(jnp.concatenate([no_shift, shift_rows[4]])[None])[0]
        chunk_rows = memory_rows.shape[2]
        source_rows = memory_rows.reshape(-1, width)
        pair_rows = (
            jnp.dot(source_rows, cross_pair, preferred_element_type=F32) + pair_shift
        ).astype(BF).reshape(CHUNKS, item_count, chunk_rows, 2 * width)
        cross_attended, cross_logs = cross_forward(memory_lengths, starts, cross_queries, pair_rows)
        cross_attended = cross_attended.reshape(row_count, width)
        cross_branch = jnp.dot(cross_attended, cross_out, preferred_element_type=F32) + shift_rows[5]
        second, second_norm_back = jax.vjp(
            layer_norm, hidden + cross_branch, gain_rows[1], shift_rows[8]
        )
        second_low = second.astype(BF)

        upward = jnp.dot(second_low, feed_up, preferred_element_type=F32) + feed_shift
        activation, gelu_back = jax.vjp(exact_gelu, upward)
        activation_low = activation.astype(BF)
        feed_branch = jnp.dot(activation_low, feed_down, preferred_element_type=F32) + shift_rows[6]
        block_out, third_norm_back = jax.vjp(
            layer_norm, second + feed_branch, gain_rows[2], shift_rows[9]
        )

        third_grad, third_gain, third_shift = third_norm_back(
            out_grad.astype(F32).reshape(row_count, width)
        )
        down_low = third_grad.astype(BF)
        grad_down = dot_tn(activation_low, down_low)
        upward_low = gelu_back(dot_nt(down_low, feed_down))[0].astype(BF)
        grad_up = dot_tn(second_low, upward_low)
        second_grad = third_grad + dot_nt(upward_low, feed_up)
        cross_grad, second_gain, second_shift = second_norm_back(second_grad)
        cross_low = cross_grad.astype(BF)
        grad_cross_out = dot_tn(cross_attended, cross_low)
        cross_incoming = dot_nt(cross_low, cross_out).astype(BF).reshape(three)
        cross_dq, pair_grad = cross_backward(
            memory_lengths, starts, cross_queries, cross_incoming, pair_rows, cross_logs
        )
        cross_query_low = cross_dq.reshape(row_count, width) * BF(query_scale)
        grad_cross_query = dot_tn(hidden_low, cross_query_low)
        flat_grad = pair_grad.reshape(-1, 2 * width)
        memory_back = dot_nt(flat_grad, cross_pair).astype(BF).reshape(memory_rows.shape)
        if tuned:
            memory_grad = join_items(exchange([memory_back[k] for k in range(8)]))
        else:
            memory_back = memory_back.swapaxes(0, 1).reshape(arrived.shape)
            memory_grad = lax.all_to_all(memory_back, "blk", split_axis=1, concat_axis=0, tiled=True)
        grad_pair = dot_tn(source_rows, flat_grad)
        value_sums = part_again(column_sum(flat_grad)[None])[0, width:]
        hidden_grad = cross_grad + dot_nt(cross_query_low, cross_query)
        first_grad, first_gain, first_shift = first_norm_back(hidden_grad)
        self_low = first_grad.astype(BF)
        grad_self_out = dot_tn(attended, self_low)
        self_incoming = dot_nt(self_low, self_out).astype(BF).reshape(three)
        joined_grad = self_backward(segment_ids, qkv, self_incoming, self_logs)
        joined_grad = joined_grad.reshape(row_count, 3 * width)
        grad_self = dot_tn(token_rows, joined_grad)
        decoder_grad = (
            (first_grad + dot_nt(joined_grad, self_proj)).astype(BF).reshape(decoder_in.shape)
        )
        joined_sums = column_sum(joined_grad)
        grad_shift_rows = jnp.stack(
            [
                joined_sums[:width],
                joined_sums[2 * width :],
                column_sum(self_low),
                column_sum(cross_query_low),
                value_sums,
                column_sum(cross_low),
                column_sum(down_low),
                first_shift,
                second_shift,
                third_shift,
            ]
        )
        grad_gain_rows = jnp.stack([first_gain, second_gain, third_gain])
        grad_feed_shift = column_sum(upward_low)
        block_low = block_out.astype(BF).reshape(decoder_in.shape)
        large = [grad_down, grad_up, grad_cross_out, grad_cross_query, grad_pair, grad_self_out, grad_self]
        if tuned:
            down, up, out, query, pair, own_out, own_in = [
                reduce_rows(grad.astype(BF), i % 2 == 1) for i, grad in enumerate(large)
            ]
            count = shifts.shape[1]
            packed = jnp.concatenate(
                [
                    grad_shift_rows.reshape(10, 8, count),
                    grad_gain_rows.reshape(3, 8, count),
                    grad_feed_shift.reshape(8, -1, count).swapaxes(0, 1),
                ],
                axis=0,
            ).swapaxes(0, 1)
            packed = jnp.pad(packed, ((0, 0), (0, 32 - packed.shape[1]), (0, 0)))
            sums = reduce_rows(packed.reshape(-1, count).astype(BF), True)
            shift_share, gain_share, feed_share = sums[:10], sums[10:13], sums[13:17].reshape(-1)
        else:
            def share(value, dim=0):
                part = lax.psum_scatter(value, "blk", scatter_dimension=dim, tiled=True)
                return lax.psum(part.astype(BF), "items").astype(F32)

            down, up, out, query, pair, own_out, own_in = [share(grad) for grad in large]
            shift_share, gain_share = share(grad_shift_rows, 1), share(grad_gain_rows, 1)
            feed_share = share(grad_feed_shift)
        return (
            block_low,
            decoder_grad,
            memory_grad,
            own_in,
            own_out,
            query,
            part_again(pair),
            out,
            up,
            down,
            shift_share,
            gain_share,
            feed_share,
        )

    return run


def solution(mesh):
    in_specs = (
        P(("items", "blk"), None, None),
        P("items", "blk", None),
        P(("items", "blk"), None),
        P(("items", "blk")),
        P("blk", None),
        P("blk", None),
        P("blk", None),
        P("blk", None),
        P("blk", None),
        P("blk", None),
        P("blk", None),
        P(None, "blk"),
        P(None, "blk"),
        P("blk"),
        P(("items", "blk"), None, None),
    )
    out_specs = (
        P(("items", "blk"), None, None),
        P(("items", "blk"), None, None),
        P("items", "blk", None),
        P("blk", None),
        P("blk", None),
        P("blk", None),
        P("blk", None),
        P("blk", None),
        P("blk", None),
        P("blk", None),
        P(None, "blk"),
        P(None, "blk"),
        P("blk"),
    )
    tuned = mesh.shape["blk"] == 8 and mesh.shape["items"] == 4
    return jax.shard_map(
        per_device(tuned), mesh=mesh, in_specs=in_specs, out_specs=out_specs, check_vma=False
    )
```

```python
import jax
import jax.numpy as jnp
from jax import lax
from jax.experimental import pallas as pl
from jax.experimental.pallas import tpu as pltpu
from jax.sharding import PartitionSpec as P

HEADS = 16
CHUNKS = 4
BF = jnp.bfloat16
F32 = jnp.float32
VMEM_BYTES = 56 * 1024 * 1024


def move(axis, pairs):
    return lambda value: lax.ppermute(value, axis, pairs)


swap_x = move("blk", [(i, i ^ 1) for i in range(8)])
swap_core = move("items", [(i, i ^ 1) for i in range(4)])
swap_y = move("items", [(i, i ^ 2) for i in range(4)])


def hop(first, last, step):
    return move("blk", [(2 * z + x, 2 * (z + step) + x) for z in range(first, last + 1) for x in (0, 1)])


def tie(value, *others):
    return lax.optimization_barrier((value,) + others)[0]


def places():
    me = lax.axis_index("blk")
    return [((me + 2 * (k // 2)) % 8) ^ (k % 2) for k in range(8)]


def spot_vector():
    group = lax.axis_index("items")
    return jnp.stack(places() + [group // 2, group % 2]).astype(jnp.int32)


def column_share(matrix, index, ways=4):
    width = matrix.shape[1] // ways
    return lax.dynamic_slice_in_dim(matrix, index * width, width, 1)


def side_by_side(matrix):
    rows = matrix.shape[0]
    if rows == 128:
        return matrix
    return jnp.concatenate([matrix[r : r + 128] for r in range(0, rows, 128)], axis=1)


ANY = pl.BlockSpec(memory_space=pl.ANY)


def place_kernel(count, extra, ways, *refs):
    spots, shards, parts = refs[0], refs[1 : 1 + count], refs[1 + count : 1 + count + 2 * ways]
    refs = refs[1 + count + 2 * ways :]
    outs, held, (in_sem, out_sem) = refs[:count], refs[count : 2 * count], refs[2 * count :]
    y, core = spots[8], spots[9]
    if ways == 2:
        shares = [core, 1 - core]
    else:
        shares = [2 * y + core, 2 * (1 - y) + core, 2 * y + 1 - core, 2 * (1 - y) + 1 - core]
    order = [1, 2, 4, 6, 3, 5, 7]
    arriving = [[] for _ in range(8)]
    used = 0

    def bring(k, source, target):
        nonlocal used
        copy = pltpu.make_async_copy(source, target, in_sem.at[used])
        copy.start()
        used += 1
        arriving[k].append(copy)

    for n in range(count):
        rows = shards[n].shape[0]
        bring(0, shards[n], held[n].at[pl.ds(pl.multiple_of(spots[0] * rows, 128), rows), :])
    for slot, k in enumerate(order):
        for c, share in enumerate(shares):
            source = parts[2 * c].at[slot] if slot < 4 else parts[2 * c + 1].at[slot - 4]
            column = 0
            for n in range(count):
                rows, columns = shards[n].shape
                if n < extra:
                    if c == 0:
                        row = pl.multiple_of(spots[k] * rows, 128)
                        bring(
                            k,
                            source.at[:, pl.ds(column, columns)],
                            held[n].at[pl.ds(row, rows), :],
                        )
                    column += columns
                    continue
                width = columns // ways
                left = pl.multiple_of(share * width, 128)
                for r in range(0, rows, 128):
                    row = pl.multiple_of(spots[k] * rows + r, 128)
                    bring(
                        k,
                        source.at[:, pl.ds(column, width)],
                        held[n].at[pl.ds(row, 128), pl.ds(left, width)],
                    )
                    column += width
    leaving = []
    for k in [0] + order:
        for copy in arriving[k]:
            copy.wait()
        for n in range(count):
            rows = shards[n].shape[0]
            span = pl.ds(pl.multiple_of(spots[k] * rows, 128), rows)
            copy = pltpu.make_async_copy(
                held[n].at[span, :], outs[n].at[span, :], out_sem.at[len(leaving)]
            )
            copy.start()
            leaving.append(copy)
    for copy in leaving:
        copy.wait()


def along_z(own, before=None):
    z = lax.axis_index("blk") // 2
    below, above = [own], [own]
    for step in range(3):
        up, down = below[-1], above[-1]
        if step == 2 and before is not None:
            up, down = tie(up, *before), tie(down, *before)
        below.append(hop(step, 2, 1)(up))
        above.append(hop(1, 3 - step, -1)(down))
    return jnp.stack([jnp.where(z + d < 4, above[d], below[4 - d]) for d in (1, 2, 3)])


def share_of(shards, ways, extra=0):
    group = lax.axis_index("items")
    index = group % 2 if ways == 2 else group
    return jnp.concatenate(
        shards[:extra] + [side_by_side(column_share(m, index, ways)) for m in shards[extra:]], axis=1
    )


def spread(shards, parts, extra=0, spots=None):
    parts = parts + [swap_core(part) for part in parts]
    ways = len(parts) // 2
    count = len(shards)
    pieces = sum(1 if n < extra else ways * shards[n].shape[0] // 128 for n in range(count))
    size = 8 * sum(m.size for m in shards)
    return pl.pallas_call(
        lambda *refs: place_kernel(count, extra, ways, *refs),
        out_shape=[jax.ShapeDtypeStruct((8 * m.shape[0], m.shape[1]), m.dtype) for m in shards],
        in_specs=[pl.BlockSpec(memory_space=pltpu.SMEM)] + [ANY] * (count + 2 * ways),
        out_specs=[ANY] * count,
        scratch_shapes=[pltpu.VMEM((8 * m.shape[0], m.shape[1]), m.dtype) for m in shards]
        + [
            pltpu.SemaphoreType.DMA((count + 7 * pieces,)),
            pltpu.SemaphoreType.DMA((8 * count,)),
        ],
        compiler_params=pltpu.CompilerParams(vmem_limit_bytes=VMEM_BYTES),
        cost_estimate=pl.CostEstimate(flops=0, bytes_accessed=4 * size, transcendentals=0),
        name="place_rows",
    )(spot_vector() if spots is None else spots, *shards, *parts)


def add_low(*terms):
    total = terms[0].astype(F32)
    for term in terms[1:]:
        total = total + term.astype(F32)
    return total.astype(BF)


class Reduce:
    def __init__(self, entries):
        group = lax.axis_index("items")
        self.y, self.core = group // 2, group % 2
        self.entries = entries
        self.shapes = []
        for entry in entries:
            rows = (entry[0] if isinstance(entry, tuple) else entry).shape[-1 if isinstance(entry, tuple) else 0]
            columns = (entry[1] if isinstance(entry, tuple) else entry).shape[1]
            self.shapes.append((rows // 8, columns))
        self.sent = [self.halves(entry, 1 - self.core) for entry in entries]
        self.got = [swap_core(v) for v in self.sent]

    def halves(self, entry, core):
        wide = entry[1] if isinstance(entry, tuple) else entry
        picked = jnp.concatenate(
            [column_share(wide, 2 * y + core) for y in (self.y, 1 - self.y)], axis=1
        )
        return dot_tn(entry[0], picked).astype(BF) if isinstance(entry, tuple) else picked

    def over_y(self):
        kept = [self.halves(entry, self.core) for entry in self.entries]

        def blocks(side):
            found = []
            for own, got in zip(kept, self.got):
                width = own.shape[1] // 2
                for left in range(side * width, (side + 1) * width, 256):
                    block = add_low(own[:, left : left + 256], got[:, left : left + 256])
                    found.append(block.reshape(8, -1, 128, 256))
            return jnp.concatenate(found, axis=1)

        self.kept, self.away = blocks(0), blocks(1)
        self.got = swap_y(self.away)
        return self.away

    def over_x(self, *before):
        me = lax.axis_index("blk")
        halves = [v.reshape((4, 2) + v.shape[1:]) for v in (self.kept, self.got)]
        away = add_low(*(lax.dynamic_index_in_dim(v, 1 - me % 2, 1, keepdims=False) for v in halves))
        if before:
            away = tie(away, *before)
        self.kept = [lax.dynamic_index_in_dim(v, me % 2, 1, keepdims=False) for v in halves]
        self.got = swap_x(away)
        return away

    def over_z(self, *before):
        z = lax.axis_index("blk") // 2
        kept = add_low(*self.kept, self.got)
        if before:
            kept = tie(kept, *before)

        def part(place):
            return lax.dynamic_index_in_dim(kept, jnp.clip(place, 0, 3), 0, keepdims=False)

        up = hop(0, 0, 1)(part(z + 3))
        down = hop(3, 3, -1)(part(z - 3))
        up = hop(0, 1, 1)(add_low(part(z + 2), up))
        down = hop(2, 3, -1)(add_low(part(z - 2), down))
        up = hop(0, 2, 1)(add_low(part(z + 1), up))
        down = hop(1, 3, -1)(add_low(part(z - 1), down))
        self.done = add_low(part(z), up, down)
        return self.done

    def share(self):
        mine = jnp.stack([self.done, swap_y(self.done)])
        every = jnp.concatenate([mine, swap_core(mine)]).astype(F32)
        ordered = [
            lax.dynamic_index_in_dim(
                every, 2 * ((q % 2) ^ self.core) + ((q // 2) ^ self.y), 0, keepdims=False
            )
            for q in range(4)
        ]
        results, first = [], 0
        for rows, columns in self.shapes:
            count = rows // 128
            strips = []
            for quarter in ordered:
                for block in range(columns // 1024):
                    place = first + block * count
                    strips.append(quarter[place : place + count].reshape(rows, 256))
            results.append(jnp.concatenate(strips, axis=1))
            first += count * (columns // 1024)
        return results


def dot_nt(left, right):
    return lax.dot_general(left, right, (((1,), (1,)), ((), ())), preferred_element_type=F32)


def dot_tn(left, right):
    return lax.dot_general(left, right, (((0,), (0,)), ((), ())), preferred_element_type=F32)


def dot_nn(left, right):
    return lax.dot_general(left, right, (((1,), (0,)), ((), ())), preferred_element_type=F32)


def two_heads(value):
    lane = lax.broadcasted_iota(jnp.int32, value.shape, 1)
    zero = jnp.zeros_like(value)
    return jnp.concatenate(
        [jnp.where(lane < 64, value, zero), jnp.where(lane < 64, zero, value)], axis=0
    )


def one_pair(turned):
    count = turned.shape[1] // 2
    joined = jnp.concatenate([turned[:64, :count], turned[64:, count:]], axis=0)
    return joined.T


def pair_forward(query, keys, values, masks):
    stacked = two_heads(query)
    scores = [mask(dot_nt(k, stacked)) for k, mask in zip(keys, masks)]
    top = scores[0].max(axis=0, keepdims=True)
    for s in scores[1:]:
        top = jnp.maximum(top, s.max(axis=0, keepdims=True))
    total, turned = None, None
    for s, v in zip(scores, values):
        weight = jnp.exp(s - top)
        add = weight.sum(axis=0, keepdims=True)
        product = dot_tn(v, weight.astype(BF))
        total = add if total is None else total + add
        turned = product if turned is None else turned + product
    return one_pair(turned * (1.0 / total)).astype(BF), top + jnp.log(total)


def pair_backward(query, incoming, keys, values, masks, log_total):
    stacked, grads = two_heads(query), two_heads(incoming)
    weights, changes, centre = [], [], None
    for k, v, mask in zip(keys, values, masks):
        weight = jnp.exp(mask(dot_nt(k, stacked)) - log_total)
        change = dot_nt(v, grads)
        add = (weight * change).sum(axis=0, keepdims=True)
        centre = add if centre is None else centre + add
        weights.append(weight)
        changes.append(change)
    key_grads, value_grads, turned = [], [], None
    for k, weight, change in zip(keys, weights, changes):
        score_grad = (weight * (change - centre)).astype(BF)
        key_grads.append(dot_nn(score_grad, stacked).astype(BF))
        value_grads.append(dot_nn(weight.astype(BF), grads).astype(BF))
        product = dot_tn(k, score_grad)
        turned = product if turned is None else turned + product
    return one_pair(turned).astype(BF), key_grads, value_grads


def slot_masks(length, rows, columns):
    slot = lax.broadcasted_iota(jnp.int32, (rows, columns), 0)
    return [
        (lambda s, c=c: jnp.where(slot < length - c * rows, s, -1e30)) for c in range(CHUNKS)
    ]


PAIRS = 4


def cross_parts(kv_ref, p):
    rows = kv_ref.shape[0] // CHUNKS
    left = 256 * p
    keys = [kv_ref[rows * c : rows * (c + 1), left : left + 128] for c in range(CHUNKS)]
    values = [kv_ref[rows * c : rows * (c + 1), left + 128 : left + 256] for c in range(CHUNKS)]
    return keys, values


def cross_forward_kernel(lengths, q_ref, m_ref, w_ref, shift_ref, out_ref, log_ref, kv_ref):
    kv_ref[...] = (dot_nn(m_ref[...], w_ref[...]) + shift_ref[...]).astype(BF)
    masks = slot_masks(lengths[0], kv_ref.shape[0] // CHUNKS, 2 * q_ref.shape[0])
    for p in range(PAIRS):
        keys, values = cross_parts(kv_ref, p)
        out, log_total = pair_forward(q_ref[:, 128 * p : 128 * p + 128], keys, values, masks)
        out_ref[:, 128 * p : 128 * p + 128] = out
        log_ref[p] = log_total


def cross_backward_kernel(
    lengths, q_ref, grad_ref, log_ref, kv_ref, w_ref, dq_ref, sum_ref, dkv_ref, back_ref, total_ref
):
    step = pl.program_id(0)
    rows = kv_ref.shape[0] // CHUNKS
    masks = slot_masks(lengths[0], rows, 2 * q_ref.shape[0])
    for p in range(PAIRS):
        span = slice(128 * p, 128 * p + 128)
        keys, values = cross_parts(kv_ref, p)
        dq, dks, dvs = pair_backward(
            q_ref[:, span], grad_ref[:, span], keys, values, masks, log_ref[p]
        )
        dq_ref[:, span] = dq
        total = None
        for c in range(CHUNKS):
            dkv_ref[rows * c : rows * (c + 1), 256 * p : 256 * p + 128] = dks[c]
            dkv_ref[rows * c : rows * (c + 1), 256 * p + 128 : 256 * p + 256] = dvs[c]
            add = dvs[c].astype(F32).sum(axis=0, keepdims=True)
            total = add if total is None else total + add
        sum_ref[:, span] = total
    back = dot_nt(dkv_ref[...], w_ref[...])

    @pl.when(step == 0)
    def _():
        total_ref[...] = back

    @pl.when(step > 0)
    def _():
        total_ref[...] += back

    @pl.when(step == pl.num_programs(0) - 1)
    def _():
        back_ref[...] = total_ref[...].astype(BF)


def cross_specs(length, slots, width):
    small = pl.BlockSpec((length, 128 * PAIRS), lambda p, *_: (0, p))
    line = pl.BlockSpec((1, 128 * PAIRS), lambda p, *_: (0, p))
    big = pl.BlockSpec((slots, 256 * PAIRS), lambda p, *_: (0, p))
    logs = pl.BlockSpec((PAIRS, 1, 2 * length), lambda p, *_: (p, 0, 0))
    whole = pl.BlockSpec((slots, width), lambda p, *_: (0, 0))
    weight = pl.BlockSpec((width, 256 * PAIRS), lambda p, *_: (0, p))
    shift = pl.BlockSpec((1, 256 * PAIRS), lambda p, *_: (0, p))
    return small, line, big, logs, whole, weight, shift


def cross_forward(lengths, queries, source, weight_pair, pair_shift):
    length, width = queries.shape
    slots = source.shape[0]
    small, _, big, logs, whole, weight, shift = cross_specs(length, slots, width)
    return pl.pallas_call(
        cross_forward_kernel,
        out_shape=[
            jax.ShapeDtypeStruct(queries.shape, BF),
            jax.ShapeDtypeStruct((width // 128, 1, 2 * length), F32),
            jax.ShapeDtypeStruct((slots, 2 * width), BF),
        ],
        grid_spec=pltpu.PrefetchScalarGridSpec(
            num_scalar_prefetch=1,
            grid=(width // (128 * PAIRS),),
            in_specs=[small, whole, weight, shift],
            out_specs=[small, logs, big],
        ),
        compiler_params=pltpu.CompilerParams(vmem_limit_bytes=VMEM_BYTES),
        cost_estimate=pl.CostEstimate(
            flops=4 * slots * width * width + 16 * length * slots * width,
            bytes_accessed=2 * (source.size + weight_pair.size + 2 * source.size),
            transcendentals=length * slots * HEADS,
        ),
        name="cross_forward",
    )(lengths, queries, source, weight_pair, pair_shift)


def cross_backward(lengths, queries, grads, logs_in, kv, weight_pair):
    length, width = queries.shape
    slots = kv.shape[0]
    small, line, big, logs, whole, weight, _ = cross_specs(length, slots, width)
    return pl.pallas_call(
        cross_backward_kernel,
        out_shape=[
            jax.ShapeDtypeStruct(queries.shape, BF),
            jax.ShapeDtypeStruct((1, width), F32),
            jax.ShapeDtypeStruct(kv.shape, BF),
            jax.ShapeDtypeStruct((slots, width), BF),
        ],
        grid_spec=pltpu.PrefetchScalarGridSpec(
            num_scalar_prefetch=1,
            grid=(width // (128 * PAIRS),),
            in_specs=[small, small, logs, big, weight],
            out_specs=[small, line, big, whole],
            scratch_shapes=[pltpu.VMEM((slots, width), F32)],
        ),
        compiler_params=pltpu.CompilerParams(vmem_limit_bytes=VMEM_BYTES),
        cost_estimate=pl.CostEstimate(
            flops=4 * slots * width * width + 40 * length * slots * width,
            bytes_accessed=2 * (4 * slots * width + 3 * slots * width + weight_pair.size),
            transcendentals=length * slots * HEADS,
        ),
        name="cross_backward",
    )(lengths, queries, grads, logs_in, kv, weight_pair)


def self_mask(seg_row, seg_column, length):
    key = lax.broadcasted_iota(jnp.int32, (length, length), 0)
    query = lax.broadcasted_iota(jnp.int32, (length, length), 1)
    allowed = jnp.where((seg_column == seg_row) & (key <= query), 1.0, 0.0)
    allowed = jnp.concatenate([allowed, allowed], axis=1)
    return lambda s: jnp.where(allowed > 0.5, s, -1e30)


def self_forward_kernel(seg_row, seg_column, qkv_ref, out_ref, log_ref):
    length, width = out_ref.shape[1:]
    mask = self_mask(seg_row[0], seg_column[0], length)
    for p in range(width // 128):
        span = slice(128 * p, 128 * p + 128)
        query = qkv_ref[0, :, span]
        key = qkv_ref[0, :, width + 128 * p : width + 128 * p + 128]
        value = qkv_ref[0, :, 2 * width + 128 * p : 2 * width + 128 * p + 128]
        out, log_total = pair_forward(query, [key], [value], [mask])
        out_ref[0, :, span] = out
        log_ref[0, p] = log_total


def self_backward_kernel(seg_row, seg_column, qkv_ref, grad_ref, log_ref, out_ref):
    length, width = grad_ref.shape[1:]
    mask = self_mask(seg_row[0], seg_column[0], length)
    for p in range(width // 128):
        span = slice(128 * p, 128 * p + 128)
        key_span = slice(width + 128 * p, width + 128 * p + 128)
        value_span = slice(2 * width + 128 * p, 2 * width + 128 * p + 128)
        dq, dk, dv = pair_backward(
            qkv_ref[0, :, span],
            grad_ref[0, :, span],
            [qkv_ref[0, :, key_span]],
            [qkv_ref[0, :, value_span]],
            [mask],
            log_ref[0, p],
        )
        out_ref[0, :, span] = dq * BF(0.125)
        out_ref[0, :, key_span] = dk[0]
        out_ref[0, :, value_span] = dv[0]


def self_specs(items, length, width):
    rows = pl.BlockSpec((1, 1, length), lambda i: (i, 0, 0))
    columns = pl.BlockSpec((1, length, 1), lambda i: (i, 0, 0))
    wide = pl.BlockSpec((1, length, 3 * width), lambda i: (i, 0, 0))
    slim = pl.BlockSpec((1, length, width), lambda i: (i, 0, 0))
    logs = pl.BlockSpec((1, width // 128, 1, 2 * length), lambda i: (i, 0, 0, 0))
    return rows, columns, wide, slim, logs


def self_forward(segments, qkv):
    items, length, width = qkv.shape[0], qkv.shape[1], qkv.shape[2] // 3
    rows, columns, wide, slim, logs = self_specs(items, length, width)
    return pl.pallas_call(
        self_forward_kernel,
        grid=(items,),
        out_shape=[
            jax.ShapeDtypeStruct((items, length, width), BF),
            jax.ShapeDtypeStruct((items, width // 128, 1, 2 * length), F32),
        ],
        in_specs=[rows, columns, wide],
        out_specs=[slim, logs],
        compiler_params=pltpu.CompilerParams(vmem_limit_bytes=VMEM_BYTES),
        name="self_forward",
    )(segments[:, None, :], segments[:, :, None], qkv)


def self_backward(segments, qkv, grads, logs_in):
    items, length, width = grads.shape
    rows, columns, wide, slim, logs = self_specs(items, length, width)
    return pl.pallas_call(
        self_backward_kernel,
        grid=(items,),
        out_shape=jax.ShapeDtypeStruct(qkv.shape, BF),
        in_specs=[rows, columns, wide, slim, logs],
        out_specs=wide,
        compiler_params=pltpu.CompilerParams(vmem_limit_bytes=VMEM_BYTES),
        name="self_backward",
    )(segments[:, None, :], segments[:, :, None], qkv, grads, logs_in)


def layer_norm(values, gain, shift):
    centre = values - jnp.mean(values, axis=-1, keepdims=True)
    spread = jnp.mean(centre * centre, axis=-1, keepdims=True)
    return centre * lax.rsqrt(spread + 1e-05) * gain + shift


def gelu_and_slope(values):
    spread = jnp.exp(-0.5 * values * values)
    t = 1.0 / (1.0 + (0.3275911 * 2.0**-0.5) * jnp.abs(values))
    tail = 1.421413741 + t * (-1.453152027 + t * 1.061405429)
    tail = 0.5 * spread * (t * (0.254829592 + t * (-0.284496736 + t * tail)))
    cdf = jnp.where(values < 0.0, tail, 1.0 - tail)
    return values * cdf, cdf + values * spread * (2.0 * jnp.pi) ** -0.5


def back_and_forth(blocks):
    return lax.all_to_all(blocks, "blk", split_axis=0, concat_axis=0, tiled=True)


def column_part(matrix, index, width):
    return lax.dynamic_slice_in_dim(matrix, index * width, width, 1)


def column_sum(values):
    return jnp.sum(values.astype(F32), axis=0)


def interleave(matrix):
    rows, columns = matrix.shape
    return matrix.reshape(rows, 2, columns // 256, 128).swapaxes(1, 2).reshape(rows, columns)


def part_again(matrix):
    rows, columns = matrix.shape
    return matrix.reshape(rows, columns // 256, 2, 128).swapaxes(1, 2).reshape(rows, columns)


def pack_small(shifts, gains, bias):
    width = shifts.shape[1]
    rows = jnp.concatenate([shifts, gains, bias.reshape(-1, width)], axis=0)
    return jnp.pad(rows, ((0, 128 - rows.shape[0]), (0, 0)))


def unpack_small(rows, width):
    rows = rows.reshape(-1, 128, width)
    shifts = rows[:, :10].transpose(1, 0, 2).reshape(10, -1)
    gains = rows[:, 10:13].transpose(1, 0, 2).reshape(3, -1)
    return shifts, gains, rows[:, 13:17].reshape(-1)


def per_device(tuned):
    def run(
        decoder_in,
        memory,
        segment_ids,
        memory_lengths,
        w_self_in,
        w_self_out,
        w_cross_query,
        w_cross_pair,
        w_cross_out,
        w_feed_up,
        w_feed_down,
        shifts,
        norm_gains,
        feed_bias,
        out_grad,
    ):
        item_count, length, width = decoder_in.shape
        row_count = item_count * length
        pair_shard = interleave(w_cross_pair)
        blocks = memory.reshape((-1, item_count) + memory.shape[1:])
        sent = [blocks[:, i] for i in range(item_count)]
        half = item_count // 2
        if tuned:
            small = pack_small(shifts, norm_gains, feed_bias)
            first = [small, w_self_in, w_self_out, w_cross_query, pair_shard]
            second = [w_cross_out, w_feed_up, w_feed_down]
            own, own_two = share_of(first, 4, 1), share_of(second, 4)
            across, across_two = swap_x(own), swap_x(own_two)
            across_y, across_two_y = swap_y(across), swap_y(across_two)
            line = along_z(own)
            own_two = tie(own_two, line, across, across_two)
            far, line_y = swap_x(line), swap_y(line)
            line_two = along_z(own_two, (far, across_y, across_two_y))
            pair = tie(jnp.stack(sent[:half], axis=1), line_two, line_y)
            pair = back_and_forth(pair)
            arrived = [pair[:, i] for i in range(half)]
            far_two, line_two_y = swap_x(line_two), swap_y(line_two)

            def near(piece, pieces):
                return jnp.concatenate([piece[None], pieces])

            small, self_proj, self_out, cross_query, cross_pair = spread(
                first, [near(across, line), far, near(across_y, line_y), swap_y(far)], 1
            )
            shift_low, gain_low, feed_shift_low = unpack_small(small, shifts.shape[1])
        else:
            def whole(shard, axis=0):
                return lax.all_gather(shard, "blk", axis=axis, tiled=True)

            shift_low, gain_low = whole(shifts, 1), whole(norm_gains, 1)
            feed_shift_low = whole(feed_bias)
            self_proj, self_out, cross_query = whole(w_self_in), whole(w_self_out), whole(w_cross_query)
            cross_pair, cross_out = whole(pair_shard), whole(w_cross_out)
            feed_up, feed_down = whole(w_feed_up), whole(w_feed_down)
            arrived = [back_and_forth(v) for v in sent]
        shift_rows = shift_low.astype(F32)
        gain_rows = gain_low.astype(F32)
        feed_shift = feed_shift_low.astype(F32)
        query_scale = (width // HEADS) ** (-0.5)
        three = (item_count, length, width)

        token_rows = decoder_in.reshape(row_count, width)
        no_shift = jnp.zeros((width,), F32)
        in_shift = jnp.concatenate([shift_rows[0], no_shift, shift_rows[1]])
        in_scale = jnp.concatenate([no_shift + query_scale, no_shift + 1.0, no_shift + 1.0])
        qkv = (
            (jnp.dot(token_rows, self_proj, preferred_element_type=F32) + in_shift) * in_scale
        ).astype(BF).reshape(item_count, length, 3 * width)
        attended, self_logs = self_forward(segment_ids, qkv)
        attended = attended.reshape(row_count, width)
        branch = jnp.dot(attended, self_out, preferred_element_type=F32) + shift_rows[2]
        hidden, first_norm_back = jax.vjp(
            layer_norm, token_rows.astype(F32) + branch, gain_rows[0], shift_rows[7]
        )
        hidden_low = hidden.astype(BF)

        cross_queries = (
            (jnp.dot(hidden_low, cross_query, preferred_element_type=F32) + shift_rows[3])
            * query_scale
        ).astype(BF).reshape(three)
        pair_shift = interleave(jnp.concatenate([no_shift, shift_rows[4]])[None])
        item_lengths = [memory_lengths[i : i + 1] for i in range(item_count)]
        sources, kvs, outs, cross_logs = [], [], [], []
        if tuned:
            far_two = tie(far_two, cross_queries)
            far_two_y = swap_y(far_two)
        for i in range(item_count):
            if tuned and i == half:
                arrived.append(back_and_forth(tie(sent[i], cross_queries, far_two, line_two_y)))
            elif tuned and i > half:
                arrived.append(
                    back_and_forth(tie(sent[i], *arrived[half:], outs[0], far_two_y))
                )
            source = arrived[i]
            if tuned and i == item_count - 1:
                parts = [near(across_two, line_two), far_two, near(across_two_y, line_two_y), far_two_y]
                cross_out, feed_up, feed_down = spread(
                    second, parts, spots=tie(spot_vector(), outs[i - 1])
                )
                source = tie(source, outs[i - 1], feed_up)
            source = source.reshape(-1, width)
            out, logs, kv = cross_forward(
                item_lengths[i], cross_queries[i], source, cross_pair, pair_shift
            )
            sources.append(source)
            kvs.append(kv)
            outs.append(out)
            cross_logs.append(logs)
        cross_attended = jnp.concatenate(outs)
        cross_branch = jnp.dot(cross_attended, cross_out, preferred_element_type=F32) + shift_rows[5]
        second, second_norm_back = jax.vjp(
            layer_norm, hidden + cross_branch, gain_rows[1], shift_rows[8]
        )
        second_low = second.astype(BF)

        upward = jnp.dot(second_low, feed_up, preferred_element_type=F32) + feed_shift
        activation, slope = gelu_and_slope(upward)
        activation_low, slope = activation.astype(BF), slope.astype(BF)
        feed_branch = jnp.dot(activation_low, feed_down, preferred_element_type=F32) + shift_rows[6]
        block_out, third_norm_back = jax.vjp(
            layer_norm, second + feed_branch, gain_rows[2], shift_rows[9]
        )

        third_grad, third_gain, third_shift = third_norm_back(
            out_grad.astype(F32).reshape(row_count, width)
        )
        down_low = third_grad.astype(BF)
        grad_down = dot_tn(activation_low, down_low)
        upward_low = (dot_nt(down_low, feed_down) * slope.astype(F32)).astype(BF)
        grad_up = dot_tn(second_low, upward_low)
        second_grad = third_grad + dot_nt(upward_low, feed_up)
        cross_grad, second_gain, second_shift = second_norm_back(second_grad)
        cross_low = cross_grad.astype(BF)
        grad_cross_out = dot_tn(cross_attended, cross_low)
        if tuned:
            sums_one = Reduce(
                [(activation_low, down_low), (second_low, upward_low), (cross_attended, cross_low)]
            )
        cross_incoming = dot_nt(cross_low, cross_out).astype(BF).reshape(three)
        if tuned:
            cross_incoming = tie(cross_incoming, *sums_one.sent)
        dqs, value_sums, grad_pair, pair_grads, memory_back, backs = [], 0.0, 0.0, [], [], []
        before = None
        for i in range(item_count):
            incoming = cross_incoming[i] if before is None else tie(cross_incoming[i], before)
            if tuned and i == 1:
                incoming = tie(incoming, sums_one.over_y())
            dq, sums, pair_grad, before = cross_backward(
                item_lengths[i], cross_queries[i], incoming, cross_logs[i], kvs[i], cross_pair
            )
            backs.append(before.reshape(arrived[i].shape))
            if len(backs) == half:
                memory_back.append(back_and_forth(jnp.stack(backs, axis=1)))
                backs = []
            value_sums = value_sums + sums[0]
            pair_grads.append(pair_grad)
            dqs.append(dq)
        cross_dq = tie(jnp.concatenate(dqs), before)
        memory_grad = jnp.concatenate(memory_back, axis=1).reshape(memory.shape)
        cross_query_low = cross_dq * BF(query_scale)
        grad_cross_query = dot_tn(hidden_low, cross_query_low)
        hidden_grad = cross_grad + dot_nt(cross_query_low, cross_query)
        first_grad, first_gain, first_shift = first_norm_back(hidden_grad)
        self_low = first_grad.astype(BF)
        grad_self_out = dot_tn(attended, self_low)
        self_incoming = dot_nt(self_low, self_out).astype(BF).reshape(three)
        joined_grad = self_backward(segment_ids, qkv, self_incoming, self_logs)
        joined_grad = joined_grad.reshape(row_count, 3 * width)
        if tuned:
            joined_grad = tie(joined_grad, sums_one.got, memory_back[0])
        grad_self = dot_tn(token_rows, joined_grad)
        decoder_grad = (
            (first_grad + dot_nt(joined_grad, self_proj)).astype(BF).reshape(decoder_in.shape)
        )
        joined_sums = column_sum(joined_grad)
        grad_shift_rows = jnp.stack(
            [
                joined_sums[:width],
                joined_sums[2 * width :],
                column_sum(self_low),
                column_sum(cross_query_low),
                value_sums,
                column_sum(cross_low),
                column_sum(down_low),
                first_shift,
                second_shift,
                third_shift,
            ]
        )
        grad_gain_rows = jnp.stack([first_gain, second_gain, third_gain])
        grad_feed_shift = column_sum(upward_low)
        block_low = block_out.astype(BF).reshape(decoder_in.shape)
        if tuned:
            count = shifts.shape[1]
            packed = jnp.concatenate(
                [
                    grad_shift_rows.reshape(10, 8, count),
                    grad_gain_rows.reshape(3, 8, count),
                    grad_feed_shift.reshape(8, -1, count).swapaxes(0, 1),
                ],
                axis=0,
            ).swapaxes(0, 1)
            packed = jnp.pad(packed, ((0, 0), (0, 128 - packed.shape[1]), (0, 7 * count)))
            sums_three = Reduce(
                [
                    (attended, self_low),
                    (token_rows, joined_grad),
                    packed.reshape(-1, 8 * count).astype(BF),
                ]
            )
            pair_grads[0] = tie(pair_grads[0], *sums_three.sent)
            away = sums_three.over_y()
            for i in range(1, item_count):
                pair_grads[i] = tie(pair_grads[i], away)
            sums_one.over_x(joined_grad)
            for source, pair_grad in zip(sources, pair_grads):
                grad_pair = grad_pair + dot_tn(source, pair_grad)
            sums_two = Reduce(
                [(hidden_low, cross_query_low), tie(grad_pair.astype(BF), sums_one.got)]
            )
            sums_two.over_y()
            sums_one.over_z(sums_two.away)
            sums_three.over_x(sums_two.away)
            sums_two.over_x()
            sums_three.over_z()
            sums_two.over_z()
            down, up, out = sums_one.share()
            (query, pair) = sums_two.share()
            (own_out, own_in, sums) = sums_three.share()
            shift_share, gain_share = sums[:10, :count], sums[10:13, :count]
            feed_share = sums[13:17, :count].reshape(-1)
        else:
            for source, pair_grad in zip(sources, pair_grads):
                grad_pair = grad_pair + dot_tn(source, pair_grad)

            def share(value, dim=0):
                part = lax.psum_scatter(value, "blk", scatter_dimension=dim, tiled=True)
                return lax.psum(part.astype(BF), "items").astype(F32)

            large = [grad_down, grad_up, grad_cross_out, grad_cross_query, grad_pair, grad_self_out, grad_self]
            down, up, out, query, pair, own_out, own_in = [share(grad) for grad in large]
            shift_share, gain_share = share(grad_shift_rows, 1), share(grad_gain_rows, 1)
            feed_share = share(grad_feed_shift)
        return (
            block_low,
            decoder_grad,
            memory_grad,
            own_in,
            own_out,
            query,
            part_again(pair),
            out,
            up,
            down,
            shift_share,
            gain_share,
            feed_share,
        )

    return run


def solution(mesh):
    in_specs = (
        P(("items", "blk"), None, None),
        P("items", "blk", None),
        P(("items", "blk"), None),
        P(("items", "blk")),
        P("blk", None),
        P("blk", None),
        P("blk", None),
        P("blk", None),
        P("blk", None),
        P("blk", None),
        P("blk", None),
        P(None, "blk"),
        P(None, "blk"),
        P("blk"),
        P(("items", "blk"), None, None),
    )
    out_specs = (
        P(("items", "blk"), None, None),
        P(("items", "blk"), None, None),
        P("items", "blk", None),
        P("blk", None),
        P("blk", None),
        P("blk", None),
        P("blk", None),
        P("blk", None),
        P("blk", None),
        P("blk", None),
        P(None, "blk"),
        P(None, "blk"),
        P("blk"),
    )
    tuned = mesh.shape["blk"] == 8 and mesh.shape["items"] == 4
    return jax.shard_map(
        per_device(tuned), mesh=mesh, in_specs=in_specs, out_specs=out_specs, check_vma=False
    )
```

```python
import jax
import jax.numpy as jnp
from jax import lax
from jax.experimental import pallas as pl
from jax.experimental.pallas import tpu as pltpu
from jax.sharding import PartitionSpec as P

HEADS = 16
CHUNKS = 4
BF = jnp.bfloat16
F32 = jnp.float32
VMEM_BYTES = 56 * 1024 * 1024


def move(axis, pairs):
    return lambda value: lax.ppermute(value, axis, pairs)


swap_x = move("blk", [(i, i ^ 1) for i in range(8)])
swap_core = move("items", [(i, i ^ 1) for i in range(4)])
swap_y = move("items", [(i, i ^ 2) for i in range(4)])


def hop(first, last, step):
    return move("blk", [(2 * z + x, 2 * (z + step) + x) for z in range(first, last + 1) for x in (0, 1)])


def tie(value, *others):
    return lax.optimization_barrier((value,) + others)[0]


def places():
    me = lax.axis_index("blk")
    return [((me + 2 * (k // 2)) % 8) ^ (k % 2) for k in range(8)]


def spot_vector():
    group = lax.axis_index("items")
    return jnp.stack(places() + [group // 2, group % 2]).astype(jnp.int32)


def column_share(matrix, index, ways=4):
    width = matrix.shape[1] // ways
    return lax.dynamic_slice_in_dim(matrix, index * width, width, 1)


def side_by_side(matrix):
    rows = matrix.shape[0]
    if rows == 128:
        return matrix
    return jnp.concatenate([matrix[r : r + 128] for r in range(0, rows, 128)], axis=1)


ANY = pl.BlockSpec(memory_space=pl.ANY)


def place_kernel(count, extra, ways, *refs):
    spots, shards, parts = refs[0], refs[1 : 1 + count], refs[1 + count : 1 + count + 2 * ways]
    refs = refs[1 + count + 2 * ways :]
    outs, held, (in_sem, out_sem) = refs[:count], refs[count : 2 * count], refs[2 * count :]
    y, core = spots[8], spots[9]
    if ways == 2:
        shares = [core, 1 - core]
    else:
        shares = [2 * y + core, 2 * (1 - y) + core, 2 * y + 1 - core, 2 * (1 - y) + 1 - core]
    order = [1, 2, 4, 6, 3, 5, 7]
    arriving = [[] for _ in range(8)]
    used = 0

    def bring(k, source, target):
        nonlocal used
        copy = pltpu.make_async_copy(source, target, in_sem.at[used])
        copy.start()
        used += 1
        arriving[k].append(copy)

    for n in range(count):
        rows = shards[n].shape[0]
        bring(0, shards[n], held[n].at[pl.ds(pl.multiple_of(spots[0] * rows, 128), rows), :])
    for slot, k in enumerate(order):
        for c, share in enumerate(shares):
            source = parts[2 * c].at[slot] if slot < 4 else parts[2 * c + 1].at[slot - 4]
            column = 0
            for n in range(count):
                rows, columns = shards[n].shape
                if n < extra:
                    if c == 0:
                        row = pl.multiple_of(spots[k] * rows, 128)
                        bring(
                            k,
                            source.at[:, pl.ds(column, columns)],
                            held[n].at[pl.ds(row, rows), :],
                        )
                    column += columns
                    continue
                width = columns // ways
                left = pl.multiple_of(share * width, 128)
                for r in range(0, rows, 128):
                    row = pl.multiple_of(spots[k] * rows + r, 128)
                    bring(
                        k,
                        source.at[:, pl.ds(column, width)],
                        held[n].at[pl.ds(row, 128), pl.ds(left, width)],
                    )
                    column += width
    leaving = []
    for k in [0] + order:
        for copy in arriving[k]:
            copy.wait()
        for n in range(count):
            rows = shards[n].shape[0]
            span = pl.ds(pl.multiple_of(spots[k] * rows, 128), rows)
            copy = pltpu.make_async_copy(
                held[n].at[span, :], outs[n].at[span, :], out_sem.at[len(leaving)]
            )
            copy.start()
            leaving.append(copy)
    for copy in leaving:
        copy.wait()


def along_z(own, before=None):
    z = lax.axis_index("blk") // 2
    below, above = [own], [own]
    for step in range(3):
        up, down = below[-1], above[-1]
        if step == 2 and before is not None:
            up, down = tie(up, *before), tie(down, *before)
        below.append(hop(step, 2, 1)(up))
        above.append(hop(1, 3 - step, -1)(down))
    return jnp.stack([jnp.where(z + d < 4, above[d], below[4 - d]) for d in (1, 2, 3)])


def share_of(shards, ways, extra=0):
    group = lax.axis_index("items")
    index = group % 2 if ways == 2 else group
    return jnp.concatenate(
        shards[:extra] + [side_by_side(column_share(m, index, ways)) for m in shards[extra:]], axis=1
    )


def spread(shards, parts, extra=0, spots=None):
    parts = parts + [swap_core(part) for part in parts]
    ways = len(parts) // 2
    count = len(shards)
    pieces = sum(1 if n < extra else ways * shards[n].shape[0] // 128 for n in range(count))
    size = 8 * sum(m.size for m in shards)
    return pl.pallas_call(
        lambda *refs: place_kernel(count, extra, ways, *refs),
        out_shape=[jax.ShapeDtypeStruct((8 * m.shape[0], m.shape[1]), m.dtype) for m in shards],
        in_specs=[pl.BlockSpec(memory_space=pltpu.SMEM)] + [ANY] * (count + 2 * ways),
        out_specs=[ANY] * count,
        scratch_shapes=[pltpu.VMEM((8 * m.shape[0], m.shape[1]), m.dtype) for m in shards]
        + [
            pltpu.SemaphoreType.DMA((count + 7 * pieces,)),
            pltpu.SemaphoreType.DMA((8 * count,)),
        ],
        compiler_params=pltpu.CompilerParams(vmem_limit_bytes=VMEM_BYTES),
        cost_estimate=pl.CostEstimate(flops=0, bytes_accessed=4 * size, transcendentals=0),
        name="place_rows",
    )(spot_vector() if spots is None else spots, *shards, *parts)


def add_low(*terms):
    total = terms[0].astype(F32)
    for term in terms[1:]:
        total = total + term.astype(F32)
    return total.astype(BF)


def in_blocks(matrix):
    return [
        matrix[:, left : left + 256].reshape(8, -1, 128, 256)
        for left in range(0, matrix.shape[1], 256)
    ]


class Reduce:
    def __init__(self, entries):
        group = lax.axis_index("items")
        self.y, self.core = group // 2, group % 2
        self.entries = entries
        self.shapes = []
        for entry in entries:
            rows = (entry[0] if isinstance(entry, tuple) else entry).shape[-1 if isinstance(entry, tuple) else 0]
            columns = (entry[1] if isinstance(entry, tuple) else entry).shape[1]
            self.shapes.append((rows // 8, columns))
        self.sent = [self.halves(entry, 1 - self.core) for entry in entries]
        self.got = [swap_core(v) for v in self.sent]

    def halves(self, entry, core):
        wide = entry[1] if isinstance(entry, tuple) else entry
        picked = jnp.concatenate(
            [column_share(wide, 2 * y + core) for y in (self.y, 1 - self.y)], axis=1
        )
        return dot_tn(entry[0], picked).astype(BF) if isinstance(entry, tuple) else picked

    def over_y(self, *before, merged=True):
        def quarter(entry, got, y, side):
            wide = entry[1] if isinstance(entry, tuple) else entry
            picked = column_share(wide, 2 * y + self.core)
            if isinstance(entry, tuple):
                picked = dot_tn(entry[0], picked)
            width = picked.shape[1]
            return add_low(picked, got[:, side * width : (side + 1) * width])

        def quarters(y, side):
            found = [quarter(entry, got, y, side) for entry, got in zip(self.entries, self.got)]
            return [jnp.concatenate([b for m in found for b in in_blocks(m)], axis=1)] if merged else found

        self.away = quarters(1 - self.y, 1)
        if before:
            self.away[0] = tie(self.away[0], *before)
        self.kept = quarters(self.y, 0)
        self.got = [swap_y(v) for v in self.away]
        return self.away

    def over_x(self, *before):
        me = lax.axis_index("blk")

        def blocks(x):
            found = []
            for kept, got in zip(self.kept, self.got):
                rows = kept.shape[0] // 8 if kept.ndim == 2 else 1
                shape = (4, 2, rows) + kept.shape[1:]
                own, came = (
                    lax.dynamic_index_in_dim(v.reshape(shape), x, 1, keepdims=False)
                    for v in (kept, got)
                )
                if kept.ndim > 2:
                    found.append(add_low(own[:, 0], came[:, 0]))
                    continue
                for left in range(0, shape[3], 256):
                    block = add_low(own[..., left : left + 256], came[..., left : left + 256])
                    found.append(block.reshape(4, -1, 128, 256))
            return found[0] if len(found) == 1 else jnp.concatenate(found, axis=1)

        away = blocks(1 - me % 2)
        if before:
            away = tie(away, *before)
        self.kept = blocks(me % 2)
        self.got = swap_x(away)
        return away

    def join(self, other):
        self.kept = jnp.concatenate([self.kept, other.kept], axis=1)
        self.got = jnp.concatenate([self.got, other.got], axis=1)
        self.shapes = self.shapes + other.shapes

    def over_z(self, first=(), second=(), third=()):
        z = lax.axis_index("blk") // 2
        kept = add_low(self.kept, self.got)

        def part(place):
            return lax.dynamic_index_in_dim(kept, jnp.clip(place, 0, 3), 0, keepdims=False)

        up = hop(0, 0, 1)(tie(part(z + 3), *first))
        down = hop(3, 3, -1)(tie(part(z - 3), *first))
        up = hop(0, 1, 1)(tie(add_low(part(z + 2), up), *second))
        down = hop(2, 3, -1)(tie(add_low(part(z - 2), down), *second))
        up = hop(0, 2, 1)(tie(add_low(part(z + 1), up), *third))
        down = hop(1, 3, -1)(tie(add_low(part(z - 1), down), *third))
        self.done = add_low(part(z), up, down)
        return self.done

    def share(self):
        mine = jnp.stack([self.done, swap_y(self.done)])
        every = jnp.concatenate([mine, swap_core(mine)]).astype(F32)
        ordered = [
            lax.dynamic_index_in_dim(
                every, 2 * ((q % 2) ^ self.core) + ((q // 2) ^ self.y), 0, keepdims=False
            )
            for q in range(4)
        ]
        results, first = [], 0
        for rows, columns in self.shapes:
            count = rows // 128
            strips = []
            for quarter in ordered:
                for block in range(columns // 1024):
                    place = first + block * count
                    strips.append(quarter[place : place + count].reshape(rows, 256))
            results.append(jnp.concatenate(strips, axis=1))
            first += count * (columns // 1024)
        return results


def dot_nt(left, right):
    return lax.dot_general(left, right, (((1,), (1,)), ((), ())), preferred_element_type=F32)


def dot_tn(left, right):
    return lax.dot_general(left, right, (((0,), (0,)), ((), ())), preferred_element_type=F32)


def dot_nn(left, right):
    return lax.dot_general(left, right, (((1,), (0,)), ((), ())), preferred_element_type=F32)


def two_heads(value):
    lane = lax.broadcasted_iota(jnp.int32, value.shape, 1)
    zero = jnp.zeros_like(value)
    return jnp.concatenate(
        [jnp.where(lane < 64, value, zero), jnp.where(lane < 64, zero, value)], axis=0
    )


def one_pair(turned):
    count = turned.shape[1] // 2
    joined = jnp.concatenate([turned[:64, :count], turned[64:, count:]], axis=0)
    return joined.T


def pair_forward(query, keys, values, masks):
    stacked = two_heads(query)
    scores = [mask(dot_nt(k, stacked)) for k, mask in zip(keys, masks)]
    top = scores[0].max(axis=0, keepdims=True)
    for s in scores[1:]:
        top = jnp.maximum(top, s.max(axis=0, keepdims=True))
    total, turned = None, None
    for s, v in zip(scores, values):
        weight = jnp.exp(s - top)
        add = weight.sum(axis=0, keepdims=True)
        product = dot_tn(v, weight.astype(BF))
        total = add if total is None else total + add
        turned = product if turned is None else turned + product
    return one_pair(turned * (1.0 / total)).astype(BF), top + jnp.log(total)


def pair_backward(query, incoming, keys, values, masks, log_total):
    stacked, grads = two_heads(query), two_heads(incoming)
    weights, changes, centre = [], [], None
    for k, v, mask in zip(keys, values, masks):
        weight = jnp.exp(mask(dot_nt(k, stacked)) - log_total)
        change = dot_nt(v, grads)
        add = (weight * change).sum(axis=0, keepdims=True)
        centre = add if centre is None else centre + add
        weights.append(weight)
        changes.append(change)
    key_grads, value_grads, turned = [], [], None
    for k, weight, change in zip(keys, weights, changes):
        score_grad = (weight * (change - centre)).astype(BF)
        key_grads.append(dot_nn(score_grad, stacked).astype(BF))
        value_grads.append(dot_nn(weight.astype(BF), grads).astype(BF))
        product = dot_tn(k, score_grad)
        turned = product if turned is None else turned + product
    return one_pair(turned).astype(BF), key_grads, value_grads


def slot_masks(length, rows, columns):
    slot = lax.broadcasted_iota(jnp.int32, (rows, columns), 0)
    return [
        (lambda s, c=c: jnp.where(slot < length - c * rows, s, -1e30)) for c in range(CHUNKS)
    ]


PAIRS = 4


def cross_parts(kv_ref, p):
    rows = kv_ref.shape[0] // CHUNKS
    left = 256 * p
    keys = [kv_ref[rows * c : rows * (c + 1), left : left + 128] for c in range(CHUNKS)]
    values = [kv_ref[rows * c : rows * (c + 1), left + 128 : left + 256] for c in range(CHUNKS)]
    return keys, values


def cross_forward_kernel(lengths, q_ref, m_ref, w_ref, shift_ref, *refs):
    out_ref, log_ref, kv_ref, all_ref = refs[-4:]

    @pl.when(pl.program_id(0) == 0)
    def _():
        all_ref[0] = m_ref[...]

    kv_ref[...] = (dot_nn(m_ref[...], w_ref[...]) + shift_ref[...]).astype(BF)
    masks = slot_masks(lengths[0], kv_ref.shape[0] // CHUNKS, 2 * q_ref.shape[0])
    for p in range(PAIRS):
        keys, values = cross_parts(kv_ref, p)
        out, log_total = pair_forward(q_ref[:, 128 * p : 128 * p + 128], keys, values, masks)
        out_ref[:, 128 * p : 128 * p + 128] = out
        log_ref[p] = log_total


def cross_backward_kernel(lengths, q_ref, grad_ref, log_ref, kv_ref, w_ref, *refs):
    dq_ref, sum_ref, dkv_ref, back_ref, total_ref = refs[-5:]
    step = pl.program_id(0)
    rows = kv_ref.shape[0] // CHUNKS
    masks = slot_masks(lengths[0], rows, 2 * q_ref.shape[0])
    for p in range(PAIRS):
        span = slice(128 * p, 128 * p + 128)
        keys, values = cross_parts(kv_ref, p)
        dq, dks, dvs = pair_backward(
            q_ref[:, span], grad_ref[:, span], keys, values, masks, log_ref[p]
        )
        dq_ref[:, span] = dq
        total = None
        for c in range(CHUNKS):
            dkv_ref[0, rows * c : rows * (c + 1), 256 * p : 256 * p + 128] = dks[c]
            dkv_ref[0, rows * c : rows * (c + 1), 256 * p + 128 : 256 * p + 256] = dvs[c]
            add = dvs[c].astype(F32).sum(axis=0, keepdims=True)
            total = add if total is None else total + add
        sum_ref[:, span] = total
    back = dot_nt(dkv_ref[0], w_ref[...])

    @pl.when(step == 0)
    def _():
        total_ref[...] = back

    @pl.when(step > 0)
    def _():
        total_ref[...] += back

    @pl.when(step == pl.num_programs(0) - 1)
    def _():
        shape = (back_ref.shape[0],) + back_ref.shape[2:]
        back_ref[:, 0] = total_ref[...].astype(BF).reshape(shape)


def cross_specs(length, slots, width):
    small = pl.BlockSpec((length, 128 * PAIRS), lambda p, *_: (0, p))
    line = pl.BlockSpec((1, 128 * PAIRS), lambda p, *_: (0, p))
    big = pl.BlockSpec((slots, 256 * PAIRS), lambda p, *_: (0, p))
    logs = pl.BlockSpec((PAIRS, 1, 2 * length), lambda p, *_: (p, 0, 0))
    whole = pl.BlockSpec((slots, width), lambda p, *_: (0, 0))
    weight = pl.BlockSpec((width, 256 * PAIRS), lambda p, *_: (0, p))
    shift = pl.BlockSpec((1, 256 * PAIRS), lambda p, *_: (0, p))
    return small, line, big, logs, whole, weight, shift


def cross_forward(lengths, queries, source, weight_pair, pair_shift, item, items, gathered):
    length, width = queries.shape
    slots = source.shape[0]
    small, _, big, logs, whole, weight, shift = cross_specs(length, slots, width)
    given = [lengths, queries, source, weight_pair, pair_shift]
    before = [] if gathered is None else [gathered]
    return pl.pallas_call(
        cross_forward_kernel,
        out_shape=[
            jax.ShapeDtypeStruct(queries.shape, BF),
            jax.ShapeDtypeStruct((width // 128, 1, 2 * length), F32),
            jax.ShapeDtypeStruct((slots, 2 * width), BF),
            jax.ShapeDtypeStruct((items, slots, width), BF),
        ],
        grid_spec=pltpu.PrefetchScalarGridSpec(
            num_scalar_prefetch=1,
            grid=(width // (128 * PAIRS),),
            in_specs=[small, whole, weight, shift] + [ANY] * len(before),
            out_specs=[small, logs, big, pl.BlockSpec((1, slots, width), lambda p, *_: (item, 0, 0))],
        ),
        input_output_aliases={5: 3} if before else {},
        compiler_params=pltpu.CompilerParams(vmem_limit_bytes=VMEM_BYTES),
        cost_estimate=pl.CostEstimate(
            flops=4 * slots * width * width + 16 * length * slots * width,
            bytes_accessed=2 * (source.size + weight_pair.size + 3 * source.size),
            transcendentals=length * slots * HEADS,
        ),
        name="cross_forward",
    )(*given, *before)


def cross_backward(lengths, queries, grads, logs_in, kv, weight_pair, item, items, dkv, back):
    length, width = queries.shape
    slots = kv.shape[0]
    small, line, big, logs, whole, weight, _ = cross_specs(length, slots, width)
    given = [lengths, queries, grads, logs_in, kv, weight_pair]
    shards, together = back[:2] if isinstance(back, tuple) else back.shape[:2]
    aliases = {}
    if not isinstance(dkv, tuple):
        aliases[len(given)] = 2
        given.append(dkv)
    if not isinstance(back, tuple):
        aliases[len(given)] = 3
        given.append(back)
    place = item % together
    return pl.pallas_call(
        cross_backward_kernel,
        out_shape=[
            jax.ShapeDtypeStruct(queries.shape, BF),
            jax.ShapeDtypeStruct((1, width), F32),
            jax.ShapeDtypeStruct((items, slots, 2 * width), BF),
            jax.ShapeDtypeStruct((shards, together, slots // shards, width), BF),
        ],
        grid_spec=pltpu.PrefetchScalarGridSpec(
            num_scalar_prefetch=1,
            grid=(width // (128 * PAIRS),),
            in_specs=[small, small, logs, big, weight] + [ANY] * len(aliases),
            out_specs=[
                small,
                line,
                pl.BlockSpec((1, slots, 256 * PAIRS), lambda p, *_: (item, 0, p)),
                pl.BlockSpec((shards, 1, slots // shards, width), lambda p, *_: (0, place, 0, 0)),
            ],
            scratch_shapes=[pltpu.VMEM((slots, width), F32)],
        ),
        input_output_aliases=aliases,
        compiler_params=pltpu.CompilerParams(vmem_limit_bytes=VMEM_BYTES),
        cost_estimate=pl.CostEstimate(
            flops=4 * slots * width * width + 40 * length * slots * width,
            bytes_accessed=2 * (4 * slots * width + 3 * slots * width + weight_pair.size),
            transcendentals=length * slots * HEADS,
        ),
        name="cross_backward",
    )(*given)


def self_mask(seg_row, seg_column, length):
    key = lax.broadcasted_iota(jnp.int32, (length, length), 0)
    query = lax.broadcasted_iota(jnp.int32, (length, length), 1)
    allowed = jnp.where((seg_column == seg_row) & (key <= query), 1.0, 0.0)
    allowed = jnp.concatenate([allowed, allowed], axis=1)
    return lambda s: jnp.where(allowed > 0.5, s, -1e30)


def self_forward_kernel(seg_row, seg_column, qkv_ref, out_ref, log_ref):
    length, width = out_ref.shape[1:]
    mask = self_mask(seg_row[0], seg_column[0], length)
    for p in range(width // 128):
        span = slice(128 * p, 128 * p + 128)
        query = qkv_ref[0, :, span]
        key = qkv_ref[0, :, width + 128 * p : width + 128 * p + 128]
        value = qkv_ref[0, :, 2 * width + 128 * p : 2 * width + 128 * p + 128]
        out, log_total = pair_forward(query, [key], [value], [mask])
        out_ref[0, :, span] = out
        log_ref[0, p] = log_total


def self_backward_kernel(seg_row, seg_column, qkv_ref, grad_ref, log_ref, out_ref):
    length, width = grad_ref.shape[1:]
    mask = self_mask(seg_row[0], seg_column[0], length)
    for p in range(width // 128):
        span = slice(128 * p, 128 * p + 128)
        key_span = slice(width + 128 * p, width + 128 * p + 128)
        value_span = slice(2 * width + 128 * p, 2 * width + 128 * p + 128)
        dq, dk, dv = pair_backward(
            qkv_ref[0, :, span],
            grad_ref[0, :, span],
            [qkv_ref[0, :, key_span]],
            [qkv_ref[0, :, value_span]],
            [mask],
            log_ref[0, p],
        )
        out_ref[0, :, span] = dq * BF(0.125)
        out_ref[0, :, key_span] = dk[0]
        out_ref[0, :, value_span] = dv[0]


def self_specs(items, length, width):
    rows = pl.BlockSpec((1, 1, length), lambda i: (i, 0, 0))
    columns = pl.BlockSpec((1, length, 1), lambda i: (i, 0, 0))
    wide = pl.BlockSpec((1, length, 3 * width), lambda i: (i, 0, 0))
    slim = pl.BlockSpec((1, length, width), lambda i: (i, 0, 0))
    logs = pl.BlockSpec((1, width // 128, 1, 2 * length), lambda i: (i, 0, 0, 0))
    return rows, columns, wide, slim, logs


def self_forward(segments, qkv):
    items, length, width = qkv.shape[0], qkv.shape[1], qkv.shape[2] // 3
    rows, columns, wide, slim, logs = self_specs(items, length, width)
    return pl.pallas_call(
        self_forward_kernel,
        grid=(items,),
        out_shape=[
            jax.ShapeDtypeStruct((items, length, width), BF),
            jax.ShapeDtypeStruct((items, width // 128, 1, 2 * length), F32),
        ],
        in_specs=[rows, columns, wide],
        out_specs=[slim, logs],
        compiler_params=pltpu.CompilerParams(vmem_limit_bytes=VMEM_BYTES),
        name="self_forward",
    )(segments[:, None, :], segments[:, :, None], qkv)


def self_backward(segments, qkv, grads, logs_in):
    items, length, width = grads.shape
    rows, columns, wide, slim, logs = self_specs(items, length, width)
    return pl.pallas_call(
        self_backward_kernel,
        grid=(items,),
        out_shape=jax.ShapeDtypeStruct(qkv.shape, BF),
        in_specs=[rows, columns, wide, slim, logs],
        out_specs=wide,
        compiler_params=pltpu.CompilerParams(vmem_limit_bytes=VMEM_BYTES),
        name="self_backward",
    )(segments[:, None, :], segments[:, :, None], qkv, grads, logs_in)


def layer_norm(values, gain, shift):
    centre = values - jnp.mean(values, axis=-1, keepdims=True)
    spread = jnp.mean(centre * centre, axis=-1, keepdims=True)
    return centre * lax.rsqrt(spread + 1e-05) * gain + shift


def gelu_and_slope(values):
    spread = jnp.exp(-0.5 * values * values)
    t = 1.0 / (1.0 + (0.3275911 * 2.0**-0.5) * jnp.abs(values))
    tail = 1.421413741 + t * (-1.453152027 + t * 1.061405429)
    tail = 0.5 * spread * (t * (0.254829592 + t * (-0.284496736 + t * tail)))
    cdf = jnp.where(values < 0.0, tail, 1.0 - tail)
    return values * cdf, cdf + values * spread * (2.0 * jnp.pi) ** -0.5


def back_and_forth(blocks):
    return lax.all_to_all(blocks, "blk", split_axis=0, concat_axis=0, tiled=True)


def column_part(matrix, index, width):
    return lax.dynamic_slice_in_dim(matrix, index * width, width, 1)


def column_sum(values):
    return dot_nn(jnp.ones((8, values.shape[0]), BF), values)[0]


def interleave(matrix):
    rows, columns = matrix.shape
    return matrix.reshape(rows, 2, columns // 256, 128).swapaxes(1, 2).reshape(rows, columns)


def part_again(matrix):
    rows, columns = matrix.shape
    return matrix.reshape(rows, columns // 256, 2, 128).swapaxes(1, 2).reshape(rows, columns)


def pack_small(shifts, gains, bias):
    width = shifts.shape[1]
    rows = jnp.concatenate([shifts, gains, bias.reshape(-1, width)], axis=0)
    return jnp.pad(rows, ((0, 128 - rows.shape[0]), (0, 0)))


def unpack_small(rows, width):
    rows = rows.reshape(-1, 128, width)
    shifts = rows[:, :10].transpose(1, 0, 2).reshape(10, -1)
    gains = rows[:, 10:13].transpose(1, 0, 2).reshape(3, -1)
    return shifts, gains, rows[:, 13:17].reshape(-1)


def per_device(tuned):
    def run(
        decoder_in,
        memory,
        segment_ids,
        memory_lengths,
        w_self_in,
        w_self_out,
        w_cross_query,
        w_cross_pair,
        w_cross_out,
        w_feed_up,
        w_feed_down,
        shifts,
        norm_gains,
        feed_bias,
        out_grad,
    ):
        item_count, length, width = decoder_in.shape
        row_count = item_count * length
        pair_shard = interleave(w_cross_pair)
        blocks = memory.reshape((-1, item_count) + memory.shape[1:])
        sent = [blocks[:, i] for i in range(item_count)]
        half = item_count // 2
        if tuned:
            small = pack_small(shifts, norm_gains, feed_bias)
            first = [small, w_self_in, w_self_out, w_cross_query, pair_shard]
            second = [w_cross_out, w_feed_up, w_feed_down]
            own, own_two = share_of(first, 4, 1), share_of(second, 4)
            across, across_two = swap_x(own), swap_x(own_two)
            across_y, across_two_y = swap_y(across), swap_y(across_two)
            line = along_z(own, (across,))
            own_two = tie(own_two, line, across_y, across_two)
            far, line_y = swap_x(line), swap_y(line)
            line_two = along_z(own_two, (far, across_two_y))
            pair = tie(jnp.stack(sent[:half], axis=1), line_two, line_y)
            pair = back_and_forth(pair)
            arrived = [pair[:, i] for i in range(half)]
            far_two, line_two_y = swap_x(line_two), swap_y(line_two)

            def near(piece, pieces):
                return jnp.concatenate([piece[None], pieces])

            small, self_proj, self_out, cross_query, cross_pair = spread(
                first, [near(across, line), far, near(across_y, line_y), swap_y(far)], 1
            )
            shift_low, gain_low, feed_shift_low = unpack_small(small, shifts.shape[1])
        else:
            def whole(shard, axis=0):
                return lax.all_gather(shard, "blk", axis=axis, tiled=True)

            shift_low, gain_low = whole(shifts, 1), whole(norm_gains, 1)
            feed_shift_low = whole(feed_bias)
            self_proj, self_out, cross_query = whole(w_self_in), whole(w_self_out), whole(w_cross_query)
            cross_pair, cross_out = whole(pair_shard), whole(w_cross_out)
            feed_up, feed_down = whole(w_feed_up), whole(w_feed_down)
            arrived = [back_and_forth(v) for v in sent]
        shift_rows = shift_low.astype(F32)
        gain_rows = gain_low.astype(F32)
        feed_shift = feed_shift_low.astype(F32)
        query_scale = (width // HEADS) ** (-0.5)
        three = (item_count, length, width)

        token_rows = decoder_in.reshape(row_count, width)
        no_shift = jnp.zeros((width,), F32)
        in_shift = jnp.concatenate([shift_rows[0], no_shift, shift_rows[1]])
        in_scale = jnp.concatenate([no_shift + query_scale, no_shift + 1.0, no_shift + 1.0])
        qkv = (
            (jnp.dot(token_rows, self_proj, preferred_element_type=F32) + in_shift) * in_scale
        ).astype(BF).reshape(item_count, length, 3 * width)
        attended, self_logs = self_forward(segment_ids, qkv)
        attended = attended.reshape(row_count, width)
        branch = jnp.dot(attended, self_out, preferred_element_type=F32) + shift_rows[2]
        hidden, first_norm_back = jax.vjp(
            layer_norm, token_rows.astype(F32) + branch, gain_rows[0], shift_rows[7]
        )
        hidden_low = hidden.astype(BF)

        cross_queries = (
            (jnp.dot(hidden_low, cross_query, preferred_element_type=F32) + shift_rows[3])
            * query_scale
        ).astype(BF).reshape(three)
        pair_shift = interleave(jnp.concatenate([no_shift, shift_rows[4]])[None])
        item_lengths = [memory_lengths[i : i + 1] for i in range(item_count)]
        gathered, kvs, outs, cross_logs = None, [], [], []
        if tuned:
            far_two = tie(far_two, cross_queries)
            far_two_y = swap_y(far_two)
        for i in range(item_count):
            if tuned and i == half:
                arrived.append(back_and_forth(tie(sent[i], cross_queries, far_two, line_two_y)))
            elif tuned and i > half:
                arrived.append(
                    back_and_forth(tie(sent[i], *arrived[half:], outs[half - 1], far_two_y))
                )
            source = arrived[i]
            if tuned and i == item_count - 1:
                parts = [near(across_two, line_two), far_two, near(across_two_y, line_two_y), far_two_y]
                cross_out, feed_up, feed_down = spread(
                    second, parts, spots=tie(spot_vector(), outs[i - 1])
                )
                source = tie(source, outs[i - 1], feed_up)
            source = source.reshape(-1, width)
            out, logs, kv, gathered = cross_forward(
                item_lengths[i], cross_queries[i], source, cross_pair, pair_shift,
                i, item_count, gathered,
            )
            kvs.append(kv)
            outs.append(out)
            cross_logs.append(logs)
        cross_attended = jnp.concatenate(outs)
        cross_branch = jnp.dot(cross_attended, cross_out, preferred_element_type=F32) + shift_rows[5]
        second, second_norm_back = jax.vjp(
            layer_norm, hidden + cross_branch, gain_rows[1], shift_rows[8]
        )
        second_low = second.astype(BF)

        upward = jnp.dot(second_low, feed_up, preferred_element_type=F32) + feed_shift
        activation, slope = gelu_and_slope(upward)
        activation_low, slope = activation.astype(BF), slope.astype(BF)
        feed_branch = jnp.dot(activation_low, feed_down, preferred_element_type=F32) + shift_rows[6]
        block_out, third_norm_back = jax.vjp(
            layer_norm, second + feed_branch, gain_rows[2], shift_rows[9]
        )

        third_grad, third_gain, third_shift = third_norm_back(
            out_grad.astype(F32).reshape(row_count, width)
        )
        down_low = third_grad.astype(BF)
        grad_down = dot_tn(activation_low, down_low)
        upward_low = (dot_nt(down_low, feed_down) * slope.astype(F32)).astype(BF)
        grad_up = dot_tn(second_low, upward_low)
        second_grad = third_grad + dot_nt(upward_low, feed_up)
        cross_grad, second_gain, second_shift = second_norm_back(second_grad)
        cross_low = cross_grad.astype(BF)
        grad_cross_out = dot_tn(cross_attended, cross_low)
        cross_incoming = dot_nt(cross_low, cross_out).astype(BF).reshape(three)
        dqs, value_sums, pair_grad, memory_back = [], 0.0, (), []
        before = None
        for i in range(item_count):
            incoming = cross_incoming[i] if before is None else tie(cross_incoming[i], before)
            if tuned and i == 1:
                lefts = [tie(v, dqs[0]) for v in (activation_low, second_low, cross_attended)]
                sums_one = Reduce(list(zip(lefts, (down_low, upward_low, cross_low))))
            if tuned and i == 2:
                incoming = tie(incoming, *sums_one.over_y(merged=False))
            if i % half == 0:
                back = (blocks.shape[0], half)
            dq, sums, pair_grad, back = cross_backward(
                item_lengths[i], cross_queries[i], incoming, cross_logs[i], kvs[i], cross_pair,
                i, item_count, pair_grad, back,
            )
            before = dq
            if i % half == half - 1:
                memory_back.append(back_and_forth(back))
            value_sums = value_sums + sums[0]
            dqs.append(dq)
        cross_dq = jnp.concatenate(dqs)
        all_sources = gathered.reshape(-1, width)
        all_grads = pair_grad.reshape(-1, 2 * width)
        memory_grad = jnp.concatenate(memory_back, axis=1).reshape(memory.shape)
        cross_query_low = cross_dq * BF(query_scale)
        grad_cross_query = dot_tn(hidden_low, cross_query_low)
        hidden_grad = cross_grad + dot_nt(cross_query_low, cross_query)
        first_grad, first_gain, first_shift = first_norm_back(hidden_grad)
        self_low = first_grad.astype(BF)
        grad_self_out = dot_tn(attended, self_low)
        self_incoming = dot_nt(self_low, self_out).astype(BF).reshape(three)
        if tuned:
            grad_pair = dot_tn(all_sources, all_grads).astype(BF)
            sums_two = Reduce([(tie(hidden_low, memory_back[0]), cross_query_low), grad_pair])
            self_incoming = tie(self_incoming, sums_one.over_x(), *sums_two.sent)
        joined_grad = self_backward(segment_ids, qkv, self_incoming, self_logs)
        joined_grad = joined_grad.reshape(row_count, 3 * width)
        if tuned:
            joined_grad = tie(joined_grad, *sums_two.over_y())
        grad_self = dot_tn(token_rows, joined_grad)
        decoder_grad = (
            (first_grad + dot_nt(joined_grad, self_proj)).astype(BF).reshape(decoder_in.shape)
        )
        joined_sums = column_sum(joined_grad)
        grad_shift_rows = jnp.stack(
            [
                joined_sums[:width],
                joined_sums[2 * width :],
                column_sum(self_low),
                column_sum(cross_query_low),
                value_sums,
                column_sum(cross_low),
                column_sum(down_low),
                first_shift,
                second_shift,
                third_shift,
            ]
        )
        grad_gain_rows = jnp.stack([first_gain, second_gain, third_gain])
        grad_feed_shift = column_sum(upward_low)
        block_low = block_out.astype(BF).reshape(decoder_in.shape)
        if tuned:
            count = shifts.shape[1]
            packed = jnp.concatenate(
                [
                    grad_shift_rows.reshape(10, 8, count),
                    grad_gain_rows.reshape(3, 8, count),
                    grad_feed_shift.reshape(8, -1, count).swapaxes(0, 1),
                ],
                axis=0,
            ).swapaxes(0, 1)
            packed = jnp.pad(packed, ((0, 0), (0, 128 - packed.shape[1]), (0, 7 * count)))
            sums_three = Reduce(
                [
                    (attended, self_low),
                    (token_rows, joined_grad),
                    packed.reshape(-1, 8 * count).astype(BF),
                ]
            )
            sums_three.over_y()
            sums_two.over_x()
            sums_three.over_x(memory_back[1])
            sums_one.over_z((), (sums_two.got,), (sums_three.got,))
            sums_three.join(sums_two)
            sums_three.over_z()
            down, up, out = sums_one.share()
            own_out, own_in, sums, query, pair = sums_three.share()
            shift_share, gain_share = sums[:10, :count], sums[10:13, :count]
            feed_share = sums[13:17, :count].reshape(-1)
        else:
            grad_pair = dot_tn(all_sources, all_grads)

            def share(value, dim=0):
                part = lax.psum_scatter(value, "blk", scatter_dimension=dim, tiled=True)
                return lax.psum(part.astype(BF), "items").astype(F32)

            large = [grad_down, grad_up, grad_cross_out, grad_cross_query, grad_pair, grad_self_out, grad_self]
            down, up, out, query, pair, own_out, own_in = [share(grad) for grad in large]
            shift_share, gain_share = share(grad_shift_rows, 1), share(grad_gain_rows, 1)
            feed_share = share(grad_feed_shift)
        return (
            block_low,
            decoder_grad,
            memory_grad,
            own_in,
            own_out,
            query,
            part_again(pair),
            out,
            up,
            down,
            shift_share,
            gain_share,
            feed_share,
        )

    return run


def solution(mesh):
    in_specs = (
        P(("items", "blk"), None, None),
        P("items", "blk", None),
        P(("items", "blk"), None),
        P(("items", "blk")),
        P("blk", None),
        P("blk", None),
        P("blk", None),
        P("blk", None),
        P("blk", None),
        P("blk", None),
        P("blk", None),
        P(None, "blk"),
        P(None, "blk"),
        P("blk"),
        P(("items", "blk"), None, None),
    )
    out_specs = (
        P(("items", "blk"), None, None),
        P(("items", "blk"), None, None),
        P("items", "blk", None),
        P("blk", None),
        P("blk", None),
        P("blk", None),
        P("blk", None),
        P("blk", None),
        P("blk", None),
        P("blk", None),
        P(None, "blk"),
        P(None, "blk"),
        P("blk"),
    )
    tuned = mesh.shape["blk"] == 8 and mesh.shape["items"] == 4
    return jax.shard_map(
        per_device(tuned), mesh=mesh, in_specs=in_specs, out_specs=out_specs, check_vma=False
    )
```

```python
import jax
import jax.numpy as jnp
from jax import lax
from jax.experimental import pallas as pl
from jax.experimental.pallas import tpu as pltpu
from jax.sharding import PartitionSpec as P

HEADS = 16
CHUNKS = 4
BF = jnp.bfloat16
F32 = jnp.float32
VMEM_BYTES = 56 * 1024 * 1024


def move(axis, pairs):
    return lambda value: lax.ppermute(value, axis, pairs)


swap_x = move("blk", [(i, i ^ 1) for i in range(8)])
swap_core = move("items", [(i, i ^ 1) for i in range(4)])
swap_y = move("items", [(i, i ^ 2) for i in range(4)])


def hop(first, last, step):
    return move("blk", [(2 * z + x, 2 * (z + step) + x) for z in range(first, last + 1) for x in (0, 1)])


def tie(value, *others):
    return lax.optimization_barrier((value,) + others)[0]


def places():
    me = lax.axis_index("blk")
    return [((me + 2 * (k // 2)) % 8) ^ (k % 2) for k in range(8)]


def spot_vector():
    group = lax.axis_index("items")
    return jnp.stack(places() + [group // 2, group % 2]).astype(jnp.int32)


def column_share(matrix, index, ways=4):
    width = matrix.shape[1] // ways
    return lax.dynamic_slice_in_dim(matrix, index * width, width, 1)


def side_by_side(matrix):
    rows = matrix.shape[0]
    if rows == 128:
        return matrix
    return jnp.concatenate([matrix[r : r + 128] for r in range(0, rows, 128)], axis=1)


ANY = pl.BlockSpec(memory_space=pl.ANY)


def place_kernel(count, extra, ways, *refs):
    spots, shards, parts = refs[0], refs[1 : 1 + count], refs[1 + count : 1 + count + 2 * ways]
    refs = refs[1 + count + 2 * ways :]
    outs, held, (in_sem, out_sem) = refs[:count], refs[count : 2 * count], refs[2 * count :]
    y, core = spots[8], spots[9]
    if ways == 2:
        shares = [core, 1 - core]
    else:
        shares = [2 * y + core, 2 * (1 - y) + core, 2 * y + 1 - core, 2 * (1 - y) + 1 - core]
    order = [1, 2, 4, 6, 3, 5, 7]
    arriving = [[] for _ in range(8)]
    used = 0

    def bring(k, source, target):
        nonlocal used
        copy = pltpu.make_async_copy(source, target, in_sem.at[used])
        copy.start()
        used += 1
        arriving[k].append(copy)

    for n in range(count):
        rows = shards[n].shape[0]
        bring(0, shards[n], held[n].at[pl.ds(pl.multiple_of(spots[0] * rows, 128), rows), :])
    for slot, k in enumerate(order):
        for c, share in enumerate(shares):
            source = parts[2 * c].at[slot] if slot < 4 else parts[2 * c + 1].at[slot - 4]
            column = 0
            for n in range(count):
                rows, columns = shards[n].shape
                if n < extra:
                    if c == 0:
                        row = pl.multiple_of(spots[k] * rows, 128)
                        bring(
                            k,
                            source.at[:, pl.ds(column, columns)],
                            held[n].at[pl.ds(row, rows), :],
                        )
                    column += columns
                    continue
                width = columns // ways
                left = pl.multiple_of(share * width, 128)
                for r in range(0, rows, 128):
                    row = pl.multiple_of(spots[k] * rows + r, 128)
                    bring(
                        k,
                        source.at[:, pl.ds(column, width)],
                        held[n].at[pl.ds(row, 128), pl.ds(left, width)],
                    )
                    column += width
    leaving = []
    for k in [0] + order:
        for copy in arriving[k]:
            copy.wait()
        for n in range(count):
            rows = shards[n].shape[0]
            span = pl.ds(pl.multiple_of(spots[k] * rows, 128), rows)
            copy = pltpu.make_async_copy(
                held[n].at[span, :], outs[n].at[span, :], out_sem.at[len(leaving)]
            )
            copy.start()
            leaving.append(copy)
    for copy in leaving:
        copy.wait()


def along_z(own, before=None):
    z = lax.axis_index("blk") // 2
    below, above = [own], [own]
    for step in range(3):
        up, down = below[-1], above[-1]
        if step == 2 and before is not None:
            up, down = tie(up, *before), tie(down, *before)
        below.append(hop(step, 2, 1)(up))
        above.append(hop(1, 3 - step, -1)(down))
    return jnp.stack([jnp.where(z + d < 4, above[d], below[4 - d]) for d in (1, 2, 3)])


def share_of(shards, ways, extra=0):
    group = lax.axis_index("items")
    index = group % 2 if ways == 2 else group
    return jnp.concatenate(
        shards[:extra] + [side_by_side(column_share(m, index, ways)) for m in shards[extra:]], axis=1
    )


def spread(shards, parts, extra=0, spots=None):
    parts = parts + [swap_core(part) for part in parts]
    ways = len(parts) // 2
    count = len(shards)
    pieces = sum(1 if n < extra else ways * shards[n].shape[0] // 128 for n in range(count))
    size = 8 * sum(m.size for m in shards)
    return pl.pallas_call(
        lambda *refs: place_kernel(count, extra, ways, *refs),
        out_shape=[jax.ShapeDtypeStruct((8 * m.shape[0], m.shape[1]), m.dtype) for m in shards],
        in_specs=[pl.BlockSpec(memory_space=pltpu.SMEM)] + [ANY] * (count + 2 * ways),
        out_specs=[ANY] * count,
        scratch_shapes=[pltpu.VMEM((8 * m.shape[0], m.shape[1]), m.dtype) for m in shards]
        + [
            pltpu.SemaphoreType.DMA((count + 7 * pieces,)),
            pltpu.SemaphoreType.DMA((8 * count,)),
        ],
        compiler_params=pltpu.CompilerParams(vmem_limit_bytes=VMEM_BYTES),
        cost_estimate=pl.CostEstimate(flops=0, bytes_accessed=4 * size, transcendentals=0),
        name="place_rows",
    )(spot_vector() if spots is None else spots, *shards, *parts)


def add_low(*terms):
    total = terms[0].astype(F32)
    for term in terms[1:]:
        total = total + term.astype(F32)
    return total.astype(BF)


def in_blocks(matrix):
    return [
        matrix[:, left : left + 256].reshape(8, -1, 128, 256)
        for left in range(0, matrix.shape[1], 256)
    ]


class Reduce:
    def __init__(self, entries):
        group = lax.axis_index("items")
        self.y, self.core = group // 2, group % 2
        self.entries = entries
        self.shapes = []
        for entry in entries:
            rows = (entry[0] if isinstance(entry, tuple) else entry).shape[-1 if isinstance(entry, tuple) else 0]
            columns = (entry[1] if isinstance(entry, tuple) else entry).shape[1]
            self.shapes.append((rows // 8, columns))
        self.sent = [self.halves(entry, 1 - self.core) for entry in entries]
        self.got = [swap_core(v) for v in self.sent]

    def halves(self, entry, core):
        wide = entry[1] if isinstance(entry, tuple) else entry
        picked = jnp.concatenate(
            [column_share(wide, 2 * y + core) for y in (self.y, 1 - self.y)], axis=1
        )
        return dot_tn(entry[0], picked).astype(BF) if isinstance(entry, tuple) else picked

    def over_y(self, *before, merged=True):
        def quarter(entry, got, y, side):
            wide = entry[1] if isinstance(entry, tuple) else entry
            picked = column_share(wide, 2 * y + self.core)
            if isinstance(entry, tuple):
                picked = dot_tn(entry[0], picked)
            width = picked.shape[1]
            return add_low(picked, got[:, side * width : (side + 1) * width])

        def quarters(y, side):
            found = [quarter(entry, got, y, side) for entry, got in zip(self.entries, self.got)]
            return [jnp.concatenate([b for m in found for b in in_blocks(m)], axis=1)] if merged else found

        self.away = quarters(1 - self.y, 1)
        if before:
            self.away[0] = tie(self.away[0], *before)
        self.kept = quarters(self.y, 0)
        self.got = [swap_y(v) for v in self.away]
        return self.away

    def over_x(self, *before):
        me = lax.axis_index("blk")

        def blocks(x):
            found = []
            for kept, got in zip(self.kept, self.got):
                rows = kept.shape[0] // 8 if kept.ndim == 2 else 1
                shape = (4, 2, rows) + kept.shape[1:]
                own, came = (
                    lax.dynamic_index_in_dim(v.reshape(shape), x, 1, keepdims=False)
                    for v in (kept, got)
                )
                if kept.ndim > 2:
                    found.append(add_low(own[:, 0], came[:, 0]))
                    continue
                for left in range(0, shape[3], 256):
                    block = add_low(own[..., left : left + 256], came[..., left : left + 256])
                    found.append(block.reshape(4, -1, 128, 256))
            return found[0] if len(found) == 1 else jnp.concatenate(found, axis=1)

        away = blocks(1 - me % 2)
        if before:
            away = tie(away, *before)
        self.kept = blocks(me % 2)
        self.got = swap_x(away)
        return away

    def join(self, other):
        self.kept = jnp.concatenate([self.kept, other.kept], axis=1)
        self.got = jnp.concatenate([self.got, other.got], axis=1)
        self.shapes = self.shapes + other.shapes

    def over_z(self, first=(), second=(), third=()):
        z = lax.axis_index("blk") // 2
        kept = add_low(self.kept, self.got)

        def part(place):
            return lax.dynamic_index_in_dim(kept, jnp.clip(place, 0, 3), 0, keepdims=False)

        up = hop(0, 0, 1)(tie(part(z + 3), *first))
        down = hop(3, 3, -1)(tie(part(z - 3), *first))
        up = hop(0, 1, 1)(tie(add_low(part(z + 2), up), *second))
        down = hop(2, 3, -1)(tie(add_low(part(z - 2), down), *second))
        up = hop(0, 2, 1)(tie(add_low(part(z + 1), up), *third))
        down = hop(1, 3, -1)(tie(add_low(part(z - 1), down), *third))
        self.done = add_low(part(z), up, down)
        return self.done

    def share(self):
        mine = jnp.stack([self.done, swap_y(self.done)])
        every = jnp.concatenate([mine, swap_core(mine)]).astype(F32)
        ordered = [
            lax.dynamic_index_in_dim(
                every, 2 * ((q % 2) ^ self.core) + ((q // 2) ^ self.y), 0, keepdims=False
            )
            for q in range(4)
        ]
        results, first = [], 0
        for rows, columns in self.shapes:
            count = rows // 128
            strips = []
            for quarter in ordered:
                for block in range(columns // 1024):
                    place = first + block * count
                    strips.append(quarter[place : place + count].reshape(rows, 256))
            results.append(jnp.concatenate(strips, axis=1))
            first += count * (columns // 1024)
        return results


def dot_nt(left, right):
    return lax.dot_general(left, right, (((1,), (1,)), ((), ())), preferred_element_type=F32)


def dot_tn(left, right):
    return lax.dot_general(left, right, (((0,), (0,)), ((), ())), preferred_element_type=F32)


def dot_nn(left, right):
    return lax.dot_general(left, right, (((1,), (0,)), ((), ())), preferred_element_type=F32)


def two_heads(value):
    lane = lax.broadcasted_iota(jnp.int32, value.shape, 1)
    zero = jnp.zeros_like(value)
    return jnp.concatenate(
        [jnp.where(lane < 64, value, zero), jnp.where(lane < 64, zero, value)], axis=0
    )


def one_pair(turned):
    count = turned.shape[1] // 2
    joined = jnp.concatenate([turned[:64, :count], turned[64:, count:]], axis=0)
    return joined.T


def pair_forward(query, keys, values, masks):
    stacked = two_heads(query)
    scores = [mask(dot_nt(k, stacked)) for k, mask in zip(keys, masks)]
    top = scores[0].max(axis=0, keepdims=True)
    for s in scores[1:]:
        top = jnp.maximum(top, s.max(axis=0, keepdims=True))
    total, turned = None, None
    for s, v in zip(scores, values):
        weight = jnp.exp(s - top)
        add = weight.sum(axis=0, keepdims=True)
        product = dot_tn(v, weight.astype(BF))
        total = add if total is None else total + add
        turned = product if turned is None else turned + product
    return one_pair(turned * (1.0 / total)).astype(BF), top + jnp.log(total)


def pair_backward(query, incoming, keys, values, masks, log_total):
    stacked, grads = two_heads(query), two_heads(incoming)
    weights, changes, centre = [], [], None
    for k, v, mask in zip(keys, values, masks):
        weight = jnp.exp(mask(dot_nt(k, stacked)) - log_total)
        change = dot_nt(v, grads)
        add = (weight * change).sum(axis=0, keepdims=True)
        centre = add if centre is None else centre + add
        weights.append(weight)
        changes.append(change)
    key_grads, value_grads, turned = [], [], None
    for k, weight, change in zip(keys, weights, changes):
        score_grad = (weight * (change - centre)).astype(BF)
        key_grads.append(dot_nn(score_grad, stacked).astype(BF))
        value_grads.append(dot_nn(weight.astype(BF), grads).astype(BF))
        product = dot_tn(k, score_grad)
        turned = product if turned is None else turned + product
    return one_pair(turned).astype(BF), key_grads, value_grads


def slot_masks(length, rows, columns):
    slot = lax.broadcasted_iota(jnp.int32, (rows, columns), 0)
    return [
        (lambda s, c=c: jnp.where(slot < length - c * rows, s, -1e30)) for c in range(CHUNKS)
    ]


PAIRS = 4


def cross_parts(kv_ref, p):
    rows = kv_ref.shape[0] // CHUNKS
    left = 256 * p
    keys = [kv_ref[rows * c : rows * (c + 1), left : left + 128] for c in range(CHUNKS)]
    values = [kv_ref[rows * c : rows * (c + 1), left + 128 : left + 256] for c in range(CHUNKS)]
    return keys, values


def cross_forward_kernel(lengths, q_ref, m_ref, w_ref, shift_ref, *refs):
    out_ref, log_ref, kv_ref, all_ref = refs[-4:]

    @pl.when(pl.program_id(0) == 0)
    def _():
        all_ref[0] = m_ref[...]

    kv_ref[...] = (dot_nn(m_ref[...], w_ref[...]) + shift_ref[...]).astype(BF)
    masks = slot_masks(lengths[0], kv_ref.shape[0] // CHUNKS, 2 * q_ref.shape[0])
    for p in range(PAIRS):
        keys, values = cross_parts(kv_ref, p)
        out, log_total = pair_forward(q_ref[:, 128 * p : 128 * p + 128], keys, values, masks)
        out_ref[:, 128 * p : 128 * p + 128] = out
        log_ref[p] = log_total


def cross_backward_kernel(lengths, q_ref, grad_ref, log_ref, kv_ref, w_ref, *refs):
    dq_ref, sum_ref, dkv_ref, back_ref, total_ref = refs[-5:]
    step = pl.program_id(0)
    rows = kv_ref.shape[0] // CHUNKS
    masks = slot_masks(lengths[0], rows, 2 * q_ref.shape[0])
    for p in range(PAIRS):
        span = slice(128 * p, 128 * p + 128)
        keys, values = cross_parts(kv_ref, p)
        dq, dks, dvs = pair_backward(
            q_ref[:, span], grad_ref[:, span], keys, values, masks, log_ref[p]
        )
        dq_ref[:, span] = dq
        total = None
        for c in range(CHUNKS):
            dkv_ref[0, rows * c : rows * (c + 1), 256 * p : 256 * p + 128] = dks[c]
            dkv_ref[0, rows * c : rows * (c + 1), 256 * p + 128 : 256 * p + 256] = dvs[c]
            add = dvs[c].astype(F32).sum(axis=0, keepdims=True)
            total = add if total is None else total + add
        sum_ref[:, span] = total
    back = dot_nt(dkv_ref[0], w_ref[...])

    @pl.when(step == 0)
    def _():
        total_ref[...] = back

    @pl.when(step > 0)
    def _():
        total_ref[...] += back

    @pl.when(step == pl.num_programs(0) - 1)
    def _():
        shape = (back_ref.shape[0],) + back_ref.shape[2:]
        back_ref[:, 0] = total_ref[...].astype(BF).reshape(shape)


def cross_specs(length, slots, width):
    small = pl.BlockSpec((length, 128 * PAIRS), lambda p, *_: (0, p))
    line = pl.BlockSpec((1, 128 * PAIRS), lambda p, *_: (0, p))
    big = pl.BlockSpec((slots, 256 * PAIRS), lambda p, *_: (0, p))
    logs = pl.BlockSpec((PAIRS, 1, 2 * length), lambda p, *_: (p, 0, 0))
    whole = pl.BlockSpec((slots, width), lambda p, *_: (0, 0))
    weight = pl.BlockSpec((width, 256 * PAIRS), lambda p, *_: (0, p))
    shift = pl.BlockSpec((1, 256 * PAIRS), lambda p, *_: (0, p))
    return small, line, big, logs, whole, weight, shift


def cross_forward(lengths, queries, source, weight_pair, pair_shift, item, items, gathered):
    length, width = queries.shape
    slots = source.shape[0]
    small, _, big, logs, whole, weight, shift = cross_specs(length, slots, width)
    given = [lengths, queries, source, weight_pair, pair_shift]
    before = [] if gathered is None else [gathered]
    return pl.pallas_call(
        cross_forward_kernel,
        out_shape=[
            jax.ShapeDtypeStruct(queries.shape, BF),
            jax.ShapeDtypeStruct((width // 128, 1, 2 * length), F32),
            jax.ShapeDtypeStruct((slots, 2 * width), BF),
            jax.ShapeDtypeStruct((items, slots, width), BF),
        ],
        grid_spec=pltpu.PrefetchScalarGridSpec(
            num_scalar_prefetch=1,
            grid=(width // (128 * PAIRS),),
            in_specs=[small, whole, weight, shift] + [ANY] * len(before),
            out_specs=[small, logs, big, pl.BlockSpec((1, slots, width), lambda p, *_: (item, 0, 0))],
        ),
        input_output_aliases={5: 3} if before else {},
        compiler_params=pltpu.CompilerParams(vmem_limit_bytes=VMEM_BYTES),
        cost_estimate=pl.CostEstimate(
            flops=4 * slots * width * width + 16 * length * slots * width,
            bytes_accessed=2 * (source.size + weight_pair.size + 3 * source.size),
            transcendentals=length * slots * HEADS,
        ),
        name="cross_forward",
    )(*given, *before)


def cross_backward(lengths, queries, grads, logs_in, kv, weight_pair, item, items, dkv, back):
    length, width = queries.shape
    slots = kv.shape[0]
    small, line, big, logs, whole, weight, _ = cross_specs(length, slots, width)
    given = [lengths, queries, grads, logs_in, kv, weight_pair]
    shards, together = back[:2] if isinstance(back, tuple) else back.shape[:2]
    aliases = {}
    if not isinstance(dkv, tuple):
        aliases[len(given)] = 2
        given.append(dkv)
    if not isinstance(back, tuple):
        aliases[len(given)] = 3
        given.append(back)
    place = item % together
    return pl.pallas_call(
        cross_backward_kernel,
        out_shape=[
            jax.ShapeDtypeStruct(queries.shape, BF),
            jax.ShapeDtypeStruct((1, width), F32),
            jax.ShapeDtypeStruct((items, slots, 2 * width), BF),
            jax.ShapeDtypeStruct((shards, together, slots // shards, width), BF),
        ],
        grid_spec=pltpu.PrefetchScalarGridSpec(
            num_scalar_prefetch=1,
            grid=(width // (128 * PAIRS),),
            in_specs=[small, small, logs, big, weight] + [ANY] * len(aliases),
            out_specs=[
                small,
                line,
                pl.BlockSpec((1, slots, 256 * PAIRS), lambda p, *_: (item, 0, p)),
                pl.BlockSpec((shards, 1, slots // shards, width), lambda p, *_: (0, place, 0, 0)),
            ],
            scratch_shapes=[pltpu.VMEM((slots, width), F32)],
        ),
        input_output_aliases=aliases,
        compiler_params=pltpu.CompilerParams(vmem_limit_bytes=VMEM_BYTES),
        cost_estimate=pl.CostEstimate(
            flops=4 * slots * width * width + 40 * length * slots * width,
            bytes_accessed=2 * (4 * slots * width + 3 * slots * width + weight_pair.size),
            transcendentals=length * slots * HEADS,
        ),
        name="cross_backward",
    )(*given)


FEED_BLOCK = 1024


def feed_backward_kernel(grad_ref, down_ref, slope_ref, up_ref, dup_ref, sum_ref, out_ref):
    low = (dot_nt(grad_ref[...], down_ref[...]) * slope_ref[...].astype(F32)).astype(BF)
    dup_ref[...] = low
    sum_ref[...] = low.astype(F32).sum(axis=0, keepdims=True)
    part = dot_nt(low, up_ref[...])

    @pl.when(pl.program_id(0) == 0)
    def _():
        out_ref[...] = part

    @pl.when(pl.program_id(0) > 0)
    def _():
        out_ref[...] += part


def feed_backward(down_low, feed_down, slope, feed_up):
    rows, width = down_low.shape
    hidden = feed_up.shape[1]
    whole = pl.BlockSpec((rows, width), lambda i: (0, 0))
    wide = pl.BlockSpec((rows, FEED_BLOCK), lambda i: (0, i))
    up = pl.BlockSpec((width, FEED_BLOCK), lambda i: (0, i))
    down = pl.BlockSpec((FEED_BLOCK, width), lambda i: (i, 0))
    line = pl.BlockSpec((1, FEED_BLOCK), lambda i: (0, i))
    return pl.pallas_call(
        feed_backward_kernel,
        grid=(hidden // FEED_BLOCK,),
        out_shape=[
            jax.ShapeDtypeStruct((rows, hidden), BF),
            jax.ShapeDtypeStruct((1, hidden), F32),
            jax.ShapeDtypeStruct((rows, width), F32),
        ],
        in_specs=[whole, down, wide, up],
        out_specs=[wide, line, whole],
        compiler_params=pltpu.CompilerParams(vmem_limit_bytes=VMEM_BYTES),
        cost_estimate=pl.CostEstimate(
            flops=4 * rows * width * hidden,
            bytes_accessed=4 * (width + rows) * hidden,
            transcendentals=0,
        ),
        name="feed_backward",
    )(down_low, feed_down, slope, feed_up)


def self_mask(seg_row, seg_column, length):
    key = lax.broadcasted_iota(jnp.int32, (length, length), 0)
    query = lax.broadcasted_iota(jnp.int32, (length, length), 1)
    allowed = jnp.where((seg_column == seg_row) & (key <= query), 1.0, 0.0)
    allowed = jnp.concatenate([allowed, allowed], axis=1)
    return lambda s: jnp.where(allowed > 0.5, s, -1e30)


def self_forward_kernel(seg_row, seg_column, qkv_ref, out_ref, log_ref):
    length, width = out_ref.shape[1:]
    mask = self_mask(seg_row[0], seg_column[0], length)
    for p in range(width // 128):
        span = slice(128 * p, 128 * p + 128)
        query = qkv_ref[0, :, span]
        key = qkv_ref[0, :, width + 128 * p : width + 128 * p + 128]
        value = qkv_ref[0, :, 2 * width + 128 * p : 2 * width + 128 * p + 128]
        out, log_total = pair_forward(query, [key], [value], [mask])
        out_ref[0, :, span] = out
        log_ref[0, p] = log_total


def self_backward_kernel(seg_row, seg_column, qkv_ref, grad_ref, log_ref, out_ref):
    length, width = grad_ref.shape[1:]
    mask = self_mask(seg_row[0], seg_column[0], length)
    for p in range(width // 128):
        span = slice(128 * p, 128 * p + 128)
        key_span = slice(width + 128 * p, width + 128 * p + 128)
        value_span = slice(2 * width + 128 * p, 2 * width + 128 * p + 128)
        dq, dk, dv = pair_backward(
            qkv_ref[0, :, span],
            grad_ref[0, :, span],
            [qkv_ref[0, :, key_span]],
            [qkv_ref[0, :, value_span]],
            [mask],
            log_ref[0, p],
        )
        out_ref[0, :, span] = dq * BF(0.125)
        out_ref[0, :, key_span] = dk[0]
        out_ref[0, :, value_span] = dv[0]


def self_specs(items, length, width):
    rows = pl.BlockSpec((1, 1, length), lambda i: (i, 0, 0))
    columns = pl.BlockSpec((1, length, 1), lambda i: (i, 0, 0))
    wide = pl.BlockSpec((1, length, 3 * width), lambda i: (i, 0, 0))
    slim = pl.BlockSpec((1, length, width), lambda i: (i, 0, 0))
    logs = pl.BlockSpec((1, width // 128, 1, 2 * length), lambda i: (i, 0, 0, 0))
    return rows, columns, wide, slim, logs


def self_forward(segments, qkv):
    items, length, width = qkv.shape[0], qkv.shape[1], qkv.shape[2] // 3
    rows, columns, wide, slim, logs = self_specs(items, length, width)
    return pl.pallas_call(
        self_forward_kernel,
        grid=(items,),
        out_shape=[
            jax.ShapeDtypeStruct((items, length, width), BF),
            jax.ShapeDtypeStruct((items, width // 128, 1, 2 * length), F32),
        ],
        in_specs=[rows, columns, wide],
        out_specs=[slim, logs],
        compiler_params=pltpu.CompilerParams(vmem_limit_bytes=VMEM_BYTES),
        name="self_forward",
    )(segments[:, None, :], segments[:, :, None], qkv)


def self_backward(segments, qkv, grads, logs_in):
    items, length, width = grads.shape
    rows, columns, wide, slim, logs = self_specs(items, length, width)
    return pl.pallas_call(
        self_backward_kernel,
        grid=(items,),
        out_shape=jax.ShapeDtypeStruct(qkv.shape, BF),
        in_specs=[rows, columns, wide, slim, logs],
        out_specs=wide,
        compiler_params=pltpu.CompilerParams(vmem_limit_bytes=VMEM_BYTES),
        name="self_backward",
    )(segments[:, None, :], segments[:, :, None], qkv, grads, logs_in)


def layer_norm(values, gain, shift):
    centre = values - jnp.mean(values, axis=-1, keepdims=True)
    spread = jnp.mean(centre * centre, axis=-1, keepdims=True)
    return centre * lax.rsqrt(spread + 1e-05) * gain + shift


def gelu_and_slope(values):
    spread = jnp.exp(-0.5 * values * values)
    t = 1.0 / (1.0 + (0.3275911 * 2.0**-0.5) * jnp.abs(values))
    tail = 1.421413741 + t * (-1.453152027 + t * 1.061405429)
    tail = 0.5 * spread * (t * (0.254829592 + t * (-0.284496736 + t * tail)))
    cdf = jnp.where(values < 0.0, tail, 1.0 - tail)
    return values * cdf, cdf + values * spread * (2.0 * jnp.pi) ** -0.5


def back_and_forth(blocks):
    return lax.all_to_all(blocks, "blk", split_axis=0, concat_axis=0, tiled=True)


def column_part(matrix, index, width):
    return lax.dynamic_slice_in_dim(matrix, index * width, width, 1)


def column_sum(values):
    return dot_nn(jnp.ones((8, values.shape[0]), BF), values)[0]


def interleave(matrix):
    rows, columns = matrix.shape
    return matrix.reshape(rows, 2, columns // 256, 128).swapaxes(1, 2).reshape(rows, columns)


def part_again(matrix):
    rows, columns = matrix.shape
    return matrix.reshape(rows, columns // 256, 2, 128).swapaxes(1, 2).reshape(rows, columns)


def pack_small(shifts, gains, bias):
    width = shifts.shape[1]
    rows = jnp.concatenate([shifts, gains, bias.reshape(-1, width)], axis=0)
    return jnp.pad(rows, ((0, 128 - rows.shape[0]), (0, 0)))


def unpack_small(rows, width):
    rows = rows.reshape(-1, 128, width)
    shifts = rows[:, :10].transpose(1, 0, 2).reshape(10, -1)
    gains = rows[:, 10:13].transpose(1, 0, 2).reshape(3, -1)
    return shifts, gains, rows[:, 13:17].reshape(-1)


def per_device(tuned):
    def run(
        decoder_in,
        memory,
        segment_ids,
        memory_lengths,
        w_self_in,
        w_self_out,
        w_cross_query,
        w_cross_pair,
        w_cross_out,
        w_feed_up,
        w_feed_down,
        shifts,
        norm_gains,
        feed_bias,
        out_grad,
    ):
        item_count, length, width = decoder_in.shape
        row_count = item_count * length
        pair_shard = interleave(w_cross_pair)
        blocks = memory.reshape((-1, item_count) + memory.shape[1:])
        sent = [blocks[:, i] for i in range(item_count)]
        half = item_count // 2
        if tuned:
            small = pack_small(shifts, norm_gains, feed_bias)
            first = [small, w_self_in, w_self_out, w_cross_query, pair_shard]
            second = [w_cross_out, w_feed_up, w_feed_down]
            own, own_two = share_of(first, 4, 1), share_of(second, 4)
            across, across_two = swap_x(own), swap_x(own_two)
            across_y, across_two_y = swap_y(across), swap_y(across_two)
            line = along_z(own, (across,))
            own_two = tie(own_two, line, across_y, across_two)
            far, line_y = swap_x(line), swap_y(line)
            line_two = along_z(own_two, (far, across_two_y))
            pair = tie(jnp.stack(sent[:half], axis=1), line_two, line_y)
            pair = back_and_forth(pair)
            arrived = [pair[:, i] for i in range(half)]
            far_two, line_two_y = swap_x(line_two), swap_y(line_two)

            def near(piece, pieces):
                return jnp.concatenate([piece[None], pieces])

            small, self_proj, self_out, cross_query, cross_pair = spread(
                first, [near(across, line), far, near(across_y, line_y), swap_y(far)], 1
            )
            shift_low, gain_low, feed_shift_low = unpack_small(small, shifts.shape[1])
        else:
            def whole(shard, axis=0):
                return lax.all_gather(shard, "blk", axis=axis, tiled=True)

            shift_low, gain_low = whole(shifts, 1), whole(norm_gains, 1)
            feed_shift_low = whole(feed_bias)
            self_proj, self_out, cross_query = whole(w_self_in), whole(w_self_out), whole(w_cross_query)
            cross_pair, cross_out = whole(pair_shard), whole(w_cross_out)
            feed_up, feed_down = whole(w_feed_up), whole(w_feed_down)
            arrived = [back_and_forth(v) for v in sent]
        shift_rows = shift_low.astype(F32)
        gain_rows = gain_low.astype(F32)
        feed_shift = feed_shift_low.astype(F32)
        query_scale = (width // HEADS) ** (-0.5)
        three = (item_count, length, width)

        token_rows = decoder_in.reshape(row_count, width)
        no_shift = jnp.zeros((width,), F32)
        in_shift = jnp.concatenate([shift_rows[0], no_shift, shift_rows[1]])
        in_scale = jnp.concatenate([no_shift + query_scale, no_shift + 1.0, no_shift + 1.0])
        qkv = (
            (jnp.dot(token_rows, self_proj, preferred_element_type=F32) + in_shift) * in_scale
        ).astype(BF).reshape(item_count, length, 3 * width)
        attended, self_logs = self_forward(segment_ids, qkv)
        attended = attended.reshape(row_count, width)
        branch = jnp.dot(attended, self_out, preferred_element_type=F32) + shift_rows[2]
        hidden, first_norm_back = jax.vjp(
            layer_norm, token_rows.astype(F32) + branch, gain_rows[0], shift_rows[7]
        )
        hidden_low = hidden.astype(BF)

        cross_queries = (
            (jnp.dot(hidden_low, cross_query, preferred_element_type=F32) + shift_rows[3])
            * query_scale
        ).astype(BF).reshape(three)
        pair_shift = interleave(jnp.concatenate([no_shift, shift_rows[4]])[None])
        item_lengths = [memory_lengths[i : i + 1] for i in range(item_count)]
        gathered, kvs, outs, cross_logs = None, [], [], []
        if tuned:
            far_two = tie(far_two, cross_queries)
            far_two_y = swap_y(far_two)
        for i in range(item_count):
            if tuned and i == half:
                arrived.append(back_and_forth(tie(sent[i], cross_queries, line_two_y)))
            elif tuned and i > half:
                arrived.append(
                    back_and_forth(tie(sent[i], *arrived[half:], outs[half - 1], far_two_y))
                )
            source = arrived[i]
            if tuned and i == item_count - 1:
                parts = [near(across_two, line_two), far_two, near(across_two_y, line_two_y), far_two_y]
                cross_out, feed_up, feed_down = spread(
                    second, parts, spots=tie(spot_vector(), outs[i - 1])
                )
                source = tie(source, outs[i - 1], feed_up)
            source = source.reshape(-1, width)
            out, logs, kv, gathered = cross_forward(
                item_lengths[i], cross_queries[i], source, cross_pair, pair_shift,
                i, item_count, gathered,
            )
            kvs.append(kv)
            outs.append(out)
            cross_logs.append(logs)
        cross_attended = jnp.concatenate(outs)
        cross_branch = jnp.dot(cross_attended, cross_out, preferred_element_type=F32) + shift_rows[5]
        second, second_norm_back = jax.vjp(
            layer_norm, hidden + cross_branch, gain_rows[1], shift_rows[8]
        )
        second_low = second.astype(BF)

        upward = jnp.dot(second_low, feed_up, preferred_element_type=F32) + feed_shift
        activation, slope = gelu_and_slope(upward)
        activation_low, slope = activation.astype(BF), slope.astype(BF)
        feed_branch = jnp.dot(activation_low, feed_down, preferred_element_type=F32) + shift_rows[6]
        block_out, third_norm_back = jax.vjp(
            layer_norm, second + feed_branch, gain_rows[2], shift_rows[9]
        )

        third_grad, third_gain, third_shift = third_norm_back(
            out_grad.astype(F32).reshape(row_count, width)
        )
        down_low = third_grad.astype(BF)
        grad_down = dot_tn(activation_low, down_low)
        upward_low, grad_feed_shift, second_grad = feed_backward(down_low, feed_down, slope, feed_up)
        grad_up = dot_tn(second_low, upward_low)
        second_grad = third_grad + second_grad
        cross_grad, second_gain, second_shift = second_norm_back(second_grad)
        cross_low = cross_grad.astype(BF)
        grad_cross_out = dot_tn(cross_attended, cross_low)
        cross_incoming = dot_nt(cross_low, cross_out).astype(BF).reshape(three)
        dqs, value_sums, pair_grad, memory_back = [], 0.0, (), []
        before = None
        for i in range(item_count):
            incoming = cross_incoming[i] if before is None else tie(cross_incoming[i], before)
            if tuned and i == 1:
                lefts = [tie(v, dqs[0]) for v in (activation_low, second_low, cross_attended)]
                sums_one = Reduce(list(zip(lefts, (down_low, upward_low, cross_low))))
            if tuned and i == 2:
                incoming = tie(incoming, *sums_one.over_y(merged=False))
            if i % half == 0:
                back = (blocks.shape[0], half)
            dq, sums, pair_grad, back = cross_backward(
                item_lengths[i], cross_queries[i], incoming, cross_logs[i], kvs[i], cross_pair,
                i, item_count, pair_grad, back,
            )
            before = dq
            if i % half == half - 1:
                memory_back.append(back_and_forth(back))
            value_sums = value_sums + sums[0]
            dqs.append(dq)
        cross_dq = jnp.concatenate(dqs)
        all_sources = gathered.reshape(-1, width)
        all_grads = pair_grad.reshape(-1, 2 * width)
        memory_grad = jnp.concatenate(memory_back, axis=1).reshape(memory.shape)
        cross_query_low = cross_dq * BF(query_scale)
        grad_cross_query = dot_tn(hidden_low, cross_query_low)
        hidden_grad = cross_grad + dot_nt(cross_query_low, cross_query)
        first_grad, first_gain, first_shift = first_norm_back(hidden_grad)
        self_low = first_grad.astype(BF)
        grad_self_out = dot_tn(attended, self_low)
        self_incoming = dot_nt(self_low, self_out).astype(BF).reshape(three)
        if tuned:
            grad_pair = dot_tn(all_sources, all_grads).astype(BF)
            sums_two = Reduce([(hidden_low, cross_query_low), tie(grad_pair, memory_back[0])])
            self_incoming = tie(self_incoming, sums_one.over_x(), *sums_two.sent)
        joined_grad = self_backward(segment_ids, qkv, self_incoming, self_logs)
        joined_grad = joined_grad.reshape(row_count, 3 * width)
        if tuned:
            joined_grad = tie(joined_grad, *sums_two.over_y())
        grad_self = dot_tn(token_rows, joined_grad)
        decoder_grad = (
            (first_grad + dot_nt(joined_grad, self_proj)).astype(BF).reshape(decoder_in.shape)
        )
        joined_sums = column_sum(joined_grad)
        grad_shift_rows = jnp.stack(
            [
                joined_sums[:width],
                joined_sums[2 * width :],
                column_sum(self_low),
                column_sum(cross_query_low),
                value_sums,
                column_sum(cross_low),
                column_sum(down_low),
                first_shift,
                second_shift,
                third_shift,
            ]
        )
        grad_gain_rows = jnp.stack([first_gain, second_gain, third_gain])
        grad_feed_shift = grad_feed_shift[0]
        block_low = block_out.astype(BF).reshape(decoder_in.shape)
        if tuned:
            count = shifts.shape[1]
            packed = jnp.concatenate(
                [
                    grad_shift_rows.reshape(10, 8, count),
                    grad_gain_rows.reshape(3, 8, count),
                    grad_feed_shift.reshape(8, -1, count).swapaxes(0, 1),
                ],
                axis=0,
            ).swapaxes(0, 1)
            packed = jnp.pad(packed, ((0, 0), (0, 128 - packed.shape[1]), (0, 7 * count)))
            sums_three = Reduce(
                [
                    (attended, self_low),
                    (token_rows, joined_grad),
                    packed.reshape(-1, 8 * count).astype(BF),
                ]
            )
            sums_three.over_y()
            sums_two.over_x()
            sums_three.over_x(memory_back[1])
            sums_one.over_z((), (sums_two.got,), (sums_three.got,))
            sums_three.join(sums_two)
            sums_three.over_z()
            down, up, out = sums_one.share()
            own_out, own_in, sums, query, pair = sums_three.share()
            shift_share, gain_share = sums[:10, :count], sums[10:13, :count]
            feed_share = sums[13:17, :count].reshape(-1)
        else:
            grad_pair = dot_tn(all_sources, all_grads)

            def share(value, dim=0):
                part = lax.psum_scatter(value, "blk", scatter_dimension=dim, tiled=True)
                return lax.psum(part.astype(BF), "items").astype(F32)

            large = [grad_down, grad_up, grad_cross_out, grad_cross_query, grad_pair, grad_self_out, grad_self]
            down, up, out, query, pair, own_out, own_in = [share(grad) for grad in large]
            shift_share, gain_share = share(grad_shift_rows, 1), share(grad_gain_rows, 1)
            feed_share = share(grad_feed_shift)
        return (
            block_low,
            decoder_grad,
            memory_grad,
            own_in,
            own_out,
            query,
            part_again(pair),
            out,
            up,
            down,
            shift_share,
            gain_share,
            feed_share,
        )

    return run


def solution(mesh):
    in_specs = (
        P(("items", "blk"), None, None),
        P("items", "blk", None),
        P(("items", "blk"), None),
        P(("items", "blk")),
        P("blk", None),
        P("blk", None),
        P("blk", None),
        P("blk", None),
        P("blk", None),
        P("blk", None),
        P("blk", None),
        P(None, "blk"),
        P(None, "blk"),
        P("blk"),
        P(("items", "blk"), None, None),
    )
    out_specs = (
        P(("items", "blk"), None, None),
        P(("items", "blk"), None, None),
        P("items", "blk", None),
        P("blk", None),
        P("blk", None),
        P("blk", None),
        P("blk", None),
        P("blk", None),
        P("blk", None),
        P("blk", None),
        P(None, "blk"),
        P(None, "blk"),
        P("blk"),
    )
    tuned = mesh.shape["blk"] == 8 and mesh.shape["items"] == 4
    return jax.shard_map(
        per_device(tuned), mesh=mesh, in_specs=in_specs, out_specs=out_specs, check_vma=False
    )
```

```python
import jax
import jax.numpy as jnp
from jax import lax
from jax.experimental import pallas as pl
from jax.experimental.pallas import tpu as pltpu
from jax.sharding import PartitionSpec as P

HEADS = 16
CHUNKS = 4
BF = jnp.bfloat16
F32 = jnp.float32
VMEM_BYTES = 56 * 1024 * 1024


def move(axis, pairs):
    return lambda value: lax.ppermute(value, axis, pairs)


swap_x = move("blk", [(i, i ^ 1) for i in range(8)])
swap_core = move("items", [(i, i ^ 1) for i in range(4)])
swap_y = move("items", [(i, i ^ 2) for i in range(4)])


def hop(first, last, step):
    return move("blk", [(2 * z + x, 2 * (z + step) + x) for z in range(first, last + 1) for x in (0, 1)])


def tie(value, *others):
    return lax.optimization_barrier((value,) + others)[0]


def places():
    me = lax.axis_index("blk")
    return [((me + 2 * (k // 2)) % 8) ^ (k % 2) for k in range(8)]


def spot_vector():
    group = lax.axis_index("items")
    return jnp.stack(places() + [group // 2, group % 2]).astype(jnp.int32)


def column_share(matrix, index, ways=4):
    width = matrix.shape[1] // ways
    return lax.dynamic_slice_in_dim(matrix, index * width, width, 1)


def side_by_side(matrix):
    rows = matrix.shape[0]
    if rows == 128:
        return matrix
    return jnp.concatenate([matrix[r : r + 128] for r in range(0, rows, 128)], axis=1)


ANY = pl.BlockSpec(memory_space=pl.ANY)


def place_kernel(count, extra, ways, *refs):
    spots, shards, parts = refs[0], refs[1 : 1 + count], refs[1 + count : 1 + count + 2 * ways]
    refs = refs[1 + count + 2 * ways :]
    outs, held, (in_sem, out_sem) = refs[:count], refs[count : 2 * count], refs[2 * count :]
    y, core = spots[8], spots[9]
    if ways == 2:
        shares = [core, 1 - core]
    else:
        shares = [2 * y + core, 2 * (1 - y) + core, 2 * y + 1 - core, 2 * (1 - y) + 1 - core]
    order = [1, 2, 4, 6, 3, 5, 7]
    arriving = [[] for _ in range(8)]
    used = 0

    def bring(k, source, target):
        nonlocal used
        copy = pltpu.make_async_copy(source, target, in_sem.at[used])
        copy.start()
        used += 1
        arriving[k].append(copy)

    for n in range(count):
        rows = shards[n].shape[0]
        bring(0, shards[n], held[n].at[pl.ds(pl.multiple_of(spots[0] * rows, 128), rows), :])
    for slot, k in enumerate(order):
        for c, share in enumerate(shares):
            source = parts[2 * c].at[slot] if slot < 4 else parts[2 * c + 1].at[slot - 4]
            column = 0
            for n in range(count):
                rows, columns = shards[n].shape
                if n < extra:
                    if c == 0:
                        row = pl.multiple_of(spots[k] * rows, 128)
                        bring(
                            k,
                            source.at[:, pl.ds(column, columns)],
                            held[n].at[pl.ds(row, rows), :],
                        )
                    column += columns
                    continue
                width = columns // ways
                left = pl.multiple_of(share * width, 128)
                for r in range(0, rows, 128):
                    row = pl.multiple_of(spots[k] * rows + r, 128)
                    bring(
                        k,
                        source.at[:, pl.ds(column, width)],
                        held[n].at[pl.ds(row, 128), pl.ds(left, width)],
                    )
                    column += width
    leaving = []
    for k in [0] + order:
        for copy in arriving[k]:
            copy.wait()
        for n in range(count):
            rows = shards[n].shape[0]
            span = pl.ds(pl.multiple_of(spots[k] * rows, 128), rows)
            copy = pltpu.make_async_copy(
                held[n].at[span, :], outs[n].at[span, :], out_sem.at[len(leaving)]
            )
            copy.start()
            leaving.append(copy)
    for copy in leaving:
        copy.wait()


def along_z(own, before=None):
    z = lax.axis_index("blk") // 2
    below, above = [own], [own]
    for step in range(3):
        up, down = below[-1], above[-1]
        if step == 2 and before is not None:
            up, down = tie(up, *before), tie(down, *before)
        below.append(hop(step, 2, 1)(up))
        above.append(hop(1, 3 - step, -1)(down))
    return jnp.stack([jnp.where(z + d < 4, above[d], below[4 - d]) for d in (1, 2, 3)])


def share_of(shards, ways, extra=0):
    group = lax.axis_index("items")
    index = group % 2 if ways == 2 else group
    return jnp.concatenate(
        shards[:extra] + [side_by_side(column_share(m, index, ways)) for m in shards[extra:]], axis=1
    )


def spread(shards, parts, extra=0, spots=None):
    parts = parts + [swap_core(part) for part in parts]
    ways = len(parts) // 2
    count = len(shards)
    pieces = sum(1 if n < extra else ways * shards[n].shape[0] // 128 for n in range(count))
    size = 8 * sum(m.size for m in shards)
    return pl.pallas_call(
        lambda *refs: place_kernel(count, extra, ways, *refs),
        out_shape=[jax.ShapeDtypeStruct((8 * m.shape[0], m.shape[1]), m.dtype) for m in shards],
        in_specs=[pl.BlockSpec(memory_space=pltpu.SMEM)] + [ANY] * (count + 2 * ways),
        out_specs=[ANY] * count,
        scratch_shapes=[pltpu.VMEM((8 * m.shape[0], m.shape[1]), m.dtype) for m in shards]
        + [
            pltpu.SemaphoreType.DMA((count + 7 * pieces,)),
            pltpu.SemaphoreType.DMA((8 * count,)),
        ],
        compiler_params=pltpu.CompilerParams(vmem_limit_bytes=VMEM_BYTES),
        cost_estimate=pl.CostEstimate(flops=0, bytes_accessed=4 * size, transcendentals=0),
        name="place_rows",
    )(spot_vector() if spots is None else spots, *shards, *parts)


def add_low(*terms):
    total = terms[0].astype(F32)
    for term in terms[1:]:
        total = total + term.astype(F32)
    return total.astype(BF)


def in_blocks(matrix):
    return [
        matrix[:, left : left + 256].reshape(8, -1, 128, 256)
        for left in range(0, matrix.shape[1], 256)
    ]


class Reduce:
    def __init__(self, entries):
        group = lax.axis_index("items")
        self.y, self.core = group // 2, group % 2
        self.entries = entries
        self.shapes = []
        for entry in entries:
            rows = (entry[0] if isinstance(entry, tuple) else entry).shape[-1 if isinstance(entry, tuple) else 0]
            columns = (entry[1] if isinstance(entry, tuple) else entry).shape[1]
            self.shapes.append((rows // 8, columns))
        self.sent = [self.halves(entry, 1 - self.core) for entry in entries]
        self.got = [swap_core(v) for v in self.sent]

    def halves(self, entry, core):
        wide = entry[1] if isinstance(entry, tuple) else entry
        picked = jnp.concatenate(
            [column_share(wide, 2 * y + core) for y in (self.y, 1 - self.y)], axis=1
        )
        return dot_tn(entry[0], picked).astype(BF) if isinstance(entry, tuple) else picked

    def over_y(self, *before, merged=True):
        def quarter(entry, got, y, side):
            wide = entry[1] if isinstance(entry, tuple) else entry
            picked = column_share(wide, 2 * y + self.core)
            if isinstance(entry, tuple):
                picked = dot_tn(entry[0], picked)
            width = picked.shape[1]
            return add_low(picked, got[:, side * width : (side + 1) * width])

        def quarters(y, side):
            found = [quarter(entry, got, y, side) for entry, got in zip(self.entries, self.got)]
            return [jnp.concatenate([b for m in found for b in in_blocks(m)], axis=1)] if merged else found

        self.away = quarters(1 - self.y, 1)
        if before:
            self.away[0] = tie(self.away[0], *before)
        self.kept = quarters(self.y, 0)
        self.got = [swap_y(v) for v in self.away]
        return self.away

    def over_x(self, *before):
        me = lax.axis_index("blk")

        def blocks(x):
            found = []
            for kept, got in zip(self.kept, self.got):
                rows = kept.shape[0] // 8 if kept.ndim == 2 else 1
                shape = (4, 2, rows) + kept.shape[1:]
                own, came = (
                    lax.dynamic_index_in_dim(v.reshape(shape), x, 1, keepdims=False)
                    for v in (kept, got)
                )
                if kept.ndim > 2:
                    found.append(add_low(own[:, 0], came[:, 0]))
                    continue
                for left in range(0, shape[3], 256):
                    block = add_low(own[..., left : left + 256], came[..., left : left + 256])
                    found.append(block.reshape(4, -1, 128, 256))
            return found[0] if len(found) == 1 else jnp.concatenate(found, axis=1)

        away = blocks(1 - me % 2)
        if before:
            away = tie(away, *before)
        self.kept = blocks(me % 2)
        self.got = swap_x(away)
        return away

    def join(self, other):
        self.kept = jnp.concatenate([self.kept, other.kept], axis=1)
        self.got = jnp.concatenate([self.got, other.got], axis=1)
        self.shapes = self.shapes + other.shapes

    def over_z(self, first=(), second=(), third=()):
        z = lax.axis_index("blk") // 2
        kept = add_low(self.kept, self.got)

        def part(place):
            return lax.dynamic_index_in_dim(kept, jnp.clip(place, 0, 3), 0, keepdims=False)

        up = hop(0, 0, 1)(tie(part(z + 3), *first))
        down = hop(3, 3, -1)(tie(part(z - 3), *first))
        up = hop(0, 1, 1)(tie(add_low(part(z + 2), up), *second))
        down = hop(2, 3, -1)(tie(add_low(part(z - 2), down), *second))
        up = hop(0, 2, 1)(tie(add_low(part(z + 1), up), *third))
        down = hop(1, 3, -1)(tie(add_low(part(z - 1), down), *third))
        self.done = add_low(part(z), up, down)
        return self.done

    def share(self):
        mine = jnp.stack([self.done, swap_y(self.done)])
        every = jnp.concatenate([mine, swap_core(mine)]).astype(F32)
        ordered = [
            lax.dynamic_index_in_dim(
                every, 2 * ((q % 2) ^ self.core) + ((q // 2) ^ self.y), 0, keepdims=False
            )
            for q in range(4)
        ]
        results, first = [], 0
        for rows, columns in self.shapes:
            count = rows // 128
            strips = []
            for quarter in ordered:
                for block in range(columns // 1024):
                    place = first + block * count
                    strips.append(quarter[place : place + count].reshape(rows, 256))
            results.append(jnp.concatenate(strips, axis=1))
            first += count * (columns // 1024)
        return results


def dot_nt(left, right):
    return lax.dot_general(left, right, (((1,), (1,)), ((), ())), preferred_element_type=F32)


def dot_tn(left, right):
    return lax.dot_general(left, right, (((0,), (0,)), ((), ())), preferred_element_type=F32)


def dot_nn(left, right):
    return lax.dot_general(left, right, (((1,), (0,)), ((), ())), preferred_element_type=F32)


def two_heads(value):
    lane = lax.broadcasted_iota(jnp.int32, value.shape, 1)
    zero = jnp.zeros_like(value)
    return jnp.concatenate(
        [jnp.where(lane < 64, value, zero), jnp.where(lane < 64, zero, value)], axis=0
    )


def one_pair(turned):
    count = turned.shape[1] // 2
    joined = jnp.concatenate([turned[:64, :count], turned[64:, count:]], axis=0)
    return joined.T


def pair_forward(query, keys, values, masks):
    stacked = two_heads(query)
    scores = [mask(dot_nt(k, stacked)) for k, mask in zip(keys, masks)]
    top = scores[0].max(axis=0, keepdims=True)
    for s in scores[1:]:
        top = jnp.maximum(top, s.max(axis=0, keepdims=True))
    total, turned = None, None
    for s, v in zip(scores, values):
        weight = jnp.exp(s - top)
        add = weight.sum(axis=0, keepdims=True)
        product = dot_tn(v, weight.astype(BF))
        total = add if total is None else total + add
        turned = product if turned is None else turned + product
    return one_pair(turned * (1.0 / total)).astype(BF), top + jnp.log(total)


def pair_backward(query, incoming, keys, values, masks, log_total):
    stacked, grads = two_heads(query), two_heads(incoming)
    weights, changes, centre = [], [], None
    for k, v, mask in zip(keys, values, masks):
        weight = jnp.exp(mask(dot_nt(k, stacked)) - log_total)
        change = dot_nt(v, grads)
        add = (weight * change).sum(axis=0, keepdims=True)
        centre = add if centre is None else centre + add
        weights.append(weight)
        changes.append(change)
    key_grads, value_grads, turned = [], [], None
    for k, weight, change in zip(keys, weights, changes):
        score_grad = (weight * (change - centre)).astype(BF)
        key_grads.append(dot_nn(score_grad, stacked).astype(BF))
        value_grads.append(dot_nn(weight.astype(BF), grads).astype(BF))
        product = dot_tn(k, score_grad)
        turned = product if turned is None else turned + product
    return one_pair(turned).astype(BF), key_grads, value_grads


def slot_masks(length, rows, columns):
    slot = lax.broadcasted_iota(jnp.int32, (rows, columns), 0)
    return [
        (lambda s, c=c: jnp.where(slot < length - c * rows, s, -1e30)) for c in range(CHUNKS)
    ]


PAIRS = 4


def cross_parts(kv_ref, p):
    rows = kv_ref.shape[0] // CHUNKS
    left = 256 * p
    keys = [kv_ref[rows * c : rows * (c + 1), left : left + 128] for c in range(CHUNKS)]
    values = [kv_ref[rows * c : rows * (c + 1), left + 128 : left + 256] for c in range(CHUNKS)]
    return keys, values


def cross_forward_kernel(lengths, q_ref, m_ref, w_ref, shift_ref, *refs):
    out_ref, log_ref, kv_ref, all_ref = refs[-4:]

    @pl.when(pl.program_id(0) == 0)
    def _():
        all_ref[0] = m_ref[...]

    kv_ref[...] = (dot_nn(m_ref[...], w_ref[...]) + shift_ref[...]).astype(BF)
    masks = slot_masks(lengths[0], kv_ref.shape[0] // CHUNKS, 2 * q_ref.shape[0])
    for p in range(PAIRS):
        keys, values = cross_parts(kv_ref, p)
        out, log_total = pair_forward(q_ref[:, 128 * p : 128 * p + 128], keys, values, masks)
        out_ref[:, 128 * p : 128 * p + 128] = out
        log_ref[p] = log_total


def cross_backward_kernel(lengths, q_ref, grad_ref, log_ref, kv_ref, w_ref, *refs):
    dq_ref, sum_ref, dkv_ref, back_ref, total_ref = refs[-5:]
    step = pl.program_id(0)
    rows = kv_ref.shape[0] // CHUNKS
    masks = slot_masks(lengths[0], rows, 2 * q_ref.shape[0])
    for p in range(PAIRS):
        span = slice(128 * p, 128 * p + 128)
        keys, values = cross_parts(kv_ref, p)
        dq, dks, dvs = pair_backward(
            q_ref[:, span], grad_ref[:, span], keys, values, masks, log_ref[p]
        )
        dq_ref[:, span] = dq
        total = None
        for c in range(CHUNKS):
            dkv_ref[0, rows * c : rows * (c + 1), 256 * p : 256 * p + 128] = dks[c]
            dkv_ref[0, rows * c : rows * (c + 1), 256 * p + 128 : 256 * p + 256] = dvs[c]
            add = dvs[c].astype(F32).sum(axis=0, keepdims=True)
            total = add if total is None else total + add
        sum_ref[:, span] = total
    back = dot_nt(dkv_ref[0], w_ref[...])

    @pl.when(step == 0)
    def _():
        total_ref[...] = back

    @pl.when(step > 0)
    def _():
        total_ref[...] += back

    @pl.when(step == pl.num_programs(0) - 1)
    def _():
        shape = (back_ref.shape[0],) + back_ref.shape[2:]
        back_ref[:, 0] = total_ref[...].astype(BF).reshape(shape)


def cross_specs(length, slots, width):
    small = pl.BlockSpec((length, 128 * PAIRS), lambda p, *_: (0, p))
    line = pl.BlockSpec((1, 128 * PAIRS), lambda p, *_: (0, p))
    big = pl.BlockSpec((slots, 256 * PAIRS), lambda p, *_: (0, p))
    logs = pl.BlockSpec((PAIRS, 1, 2 * length), lambda p, *_: (p, 0, 0))
    whole = pl.BlockSpec((slots, width), lambda p, *_: (0, 0))
    weight = pl.BlockSpec((width, 256 * PAIRS), lambda p, *_: (0, p))
    shift = pl.BlockSpec((1, 256 * PAIRS), lambda p, *_: (0, p))
    return small, line, big, logs, whole, weight, shift


def cross_forward(lengths, queries, source, weight_pair, pair_shift, item, items, gathered):
    length, width = queries.shape
    slots = source.shape[0]
    small, _, big, logs, whole, weight, shift = cross_specs(length, slots, width)
    given = [lengths, queries, source, weight_pair, pair_shift]
    before = [] if gathered is None else [gathered]
    return pl.pallas_call(
        cross_forward_kernel,
        out_shape=[
            jax.ShapeDtypeStruct(queries.shape, BF),
            jax.ShapeDtypeStruct((width // 128, 1, 2 * length), F32),
            jax.ShapeDtypeStruct((slots, 2 * width), BF),
            jax.ShapeDtypeStruct((items, slots, width), BF),
        ],
        grid_spec=pltpu.PrefetchScalarGridSpec(
            num_scalar_prefetch=1,
            grid=(width // (128 * PAIRS),),
            in_specs=[small, whole, weight, shift] + [ANY] * len(before),
            out_specs=[small, logs, big, pl.BlockSpec((1, slots, width), lambda p, *_: (item, 0, 0))],
        ),
        input_output_aliases={5: 3} if before else {},
        compiler_params=pltpu.CompilerParams(vmem_limit_bytes=VMEM_BYTES),
        cost_estimate=pl.CostEstimate(
            flops=4 * slots * width * width + 16 * length * slots * width,
            bytes_accessed=2 * (source.size + weight_pair.size + 3 * source.size),
            transcendentals=length * slots * HEADS,
        ),
        name="cross_forward",
    )(*given, *before)


def cross_backward(lengths, queries, grads, logs_in, kv, weight_pair, item, items, dkv, back):
    length, width = queries.shape
    slots = kv.shape[0]
    small, line, big, logs, whole, weight, _ = cross_specs(length, slots, width)
    given = [lengths, queries, grads, logs_in, kv, weight_pair]
    shards, together = back[:2] if isinstance(back, tuple) else back.shape[:2]
    aliases = {}
    if not isinstance(dkv, tuple):
        aliases[len(given)] = 2
        given.append(dkv)
    if not isinstance(back, tuple):
        aliases[len(given)] = 3
        given.append(back)
    place = item % together
    return pl.pallas_call(
        cross_backward_kernel,
        out_shape=[
            jax.ShapeDtypeStruct(queries.shape, BF),
            jax.ShapeDtypeStruct((1, width), F32),
            jax.ShapeDtypeStruct((items, slots, 2 * width), BF),
            jax.ShapeDtypeStruct((shards, together, slots // shards, width), BF),
        ],
        grid_spec=pltpu.PrefetchScalarGridSpec(
            num_scalar_prefetch=1,
            grid=(width // (128 * PAIRS),),
            in_specs=[small, small, logs, big, weight] + [ANY] * len(aliases),
            out_specs=[
                small,
                line,
                pl.BlockSpec((1, slots, 256 * PAIRS), lambda p, *_: (item, 0, p)),
                pl.BlockSpec((shards, 1, slots // shards, width), lambda p, *_: (0, place, 0, 0)),
            ],
            scratch_shapes=[pltpu.VMEM((slots, width), F32)],
        ),
        input_output_aliases=aliases,
        compiler_params=pltpu.CompilerParams(vmem_limit_bytes=VMEM_BYTES),
        cost_estimate=pl.CostEstimate(
            flops=4 * slots * width * width + 40 * length * slots * width,
            bytes_accessed=2 * (4 * slots * width + 3 * slots * width + weight_pair.size),
            transcendentals=length * slots * HEADS,
        ),
        name="cross_backward",
    )(*given)


FEED_BLOCK = 1024


def feed_backward_kernel(grad_ref, down_ref, slope_ref, up_ref, dup_ref, sum_ref, out_ref):
    low = (dot_nt(grad_ref[...], down_ref[...]) * slope_ref[...].astype(F32)).astype(BF)
    dup_ref[...] = low
    sum_ref[...] = low.astype(F32).sum(axis=0, keepdims=True)
    part = dot_nt(low, up_ref[...])

    @pl.when(pl.program_id(0) == 0)
    def _():
        out_ref[...] = part

    @pl.when(pl.program_id(0) > 0)
    def _():
        out_ref[...] += part


def feed_backward(down_low, feed_down, slope, feed_up):
    rows, width = down_low.shape
    hidden = feed_up.shape[1]
    whole = pl.BlockSpec((rows, width), lambda i: (0, 0))
    wide = pl.BlockSpec((rows, FEED_BLOCK), lambda i: (0, i))
    up = pl.BlockSpec((width, FEED_BLOCK), lambda i: (0, i))
    down = pl.BlockSpec((FEED_BLOCK, width), lambda i: (i, 0))
    line = pl.BlockSpec((1, FEED_BLOCK), lambda i: (0, i))
    return pl.pallas_call(
        feed_backward_kernel,
        grid=(hidden // FEED_BLOCK,),
        out_shape=[
            jax.ShapeDtypeStruct((rows, hidden), BF),
            jax.ShapeDtypeStruct((1, hidden), F32),
            jax.ShapeDtypeStruct((rows, width), F32),
        ],
        in_specs=[whole, down, wide, up],
        out_specs=[wide, line, whole],
        compiler_params=pltpu.CompilerParams(vmem_limit_bytes=VMEM_BYTES),
        cost_estimate=pl.CostEstimate(
            flops=4 * rows * width * hidden,
            bytes_accessed=4 * (width + rows) * hidden,
            transcendentals=0,
        ),
        name="feed_backward",
    )(down_low, feed_down, slope, feed_up)


def self_mask(seg_row, seg_column, length):
    key = lax.broadcasted_iota(jnp.int32, (length, length), 0)
    query = lax.broadcasted_iota(jnp.int32, (length, length), 1)
    allowed = jnp.where((seg_column == seg_row) & (key <= query), 1.0, 0.0)
    allowed = jnp.concatenate([allowed, allowed], axis=1)
    return lambda s: jnp.where(allowed > 0.5, s, -1e30)


def self_forward_kernel(seg_row, seg_column, qkv_ref, out_ref, log_ref):
    length, width = out_ref.shape[1:]
    mask = self_mask(seg_row[0], seg_column[0], length)
    for p in range(width // 128):
        span = slice(128 * p, 128 * p + 128)
        query = qkv_ref[0, :, span]
        key = qkv_ref[0, :, width + 128 * p : width + 128 * p + 128]
        value = qkv_ref[0, :, 2 * width + 128 * p : 2 * width + 128 * p + 128]
        out, log_total = pair_forward(query, [key], [value], [mask])
        out_ref[0, :, span] = out
        log_ref[0, p] = log_total


def self_backward_kernel(seg_row, seg_column, qkv_ref, grad_ref, log_ref, out_ref):
    length, width = grad_ref.shape[1:]
    mask = self_mask(seg_row[0], seg_column[0], length)
    for p in range(width // 128):
        span = slice(128 * p, 128 * p + 128)
        key_span = slice(width + 128 * p, width + 128 * p + 128)
        value_span = slice(2 * width + 128 * p, 2 * width + 128 * p + 128)
        dq, dk, dv = pair_backward(
            qkv_ref[0, :, span],
            grad_ref[0, :, span],
            [qkv_ref[0, :, key_span]],
            [qkv_ref[0, :, value_span]],
            [mask],
            log_ref[0, p],
        )
        out_ref[0, :, span] = dq * BF(0.125)
        out_ref[0, :, key_span] = dk[0]
        out_ref[0, :, value_span] = dv[0]


def self_specs(items, length, width):
    rows = pl.BlockSpec((1, 1, length), lambda i: (i, 0, 0))
    columns = pl.BlockSpec((1, length, 1), lambda i: (i, 0, 0))
    wide = pl.BlockSpec((1, length, 3 * width), lambda i: (i, 0, 0))
    slim = pl.BlockSpec((1, length, width), lambda i: (i, 0, 0))
    logs = pl.BlockSpec((1, width // 128, 1, 2 * length), lambda i: (i, 0, 0, 0))
    return rows, columns, wide, slim, logs


def self_forward(segments, qkv):
    items, length, width = qkv.shape[0], qkv.shape[1], qkv.shape[2] // 3
    rows, columns, wide, slim, logs = self_specs(items, length, width)
    return pl.pallas_call(
        self_forward_kernel,
        grid=(items,),
        out_shape=[
            jax.ShapeDtypeStruct((items, length, width), BF),
            jax.ShapeDtypeStruct((items, width // 128, 1, 2 * length), F32),
        ],
        in_specs=[rows, columns, wide],
        out_specs=[slim, logs],
        compiler_params=pltpu.CompilerParams(vmem_limit_bytes=VMEM_BYTES),
        name="self_forward",
    )(segments[:, None, :], segments[:, :, None], qkv)


def self_backward(segments, qkv, grads, logs_in):
    items, length, width = grads.shape
    rows, columns, wide, slim, logs = self_specs(items, length, width)
    return pl.pallas_call(
        self_backward_kernel,
        grid=(items,),
        out_shape=jax.ShapeDtypeStruct(qkv.shape, BF),
        in_specs=[rows, columns, wide, slim, logs],
        out_specs=wide,
        compiler_params=pltpu.CompilerParams(vmem_limit_bytes=VMEM_BYTES),
        name="self_backward",
    )(segments[:, None, :], segments[:, :, None], qkv, grads, logs_in)


def layer_norm(values, gain, shift):
    centre = values - jnp.mean(values, axis=-1, keepdims=True)
    spread = jnp.mean(centre * centre, axis=-1, keepdims=True)
    return centre * lax.rsqrt(spread + 1e-05) * gain + shift


def gelu_and_slope(values):
    spread = jnp.exp(-0.5 * values * values)
    t = 1.0 / (1.0 + (0.3275911 * 2.0**-0.5) * jnp.abs(values))
    tail = 1.421413741 + t * (-1.453152027 + t * 1.061405429)
    tail = 0.5 * spread * (t * (0.254829592 + t * (-0.284496736 + t * tail)))
    cdf = jnp.where(values < 0.0, tail, 1.0 - tail)
    return values * cdf, cdf + values * spread * (2.0 * jnp.pi) ** -0.5


def back_and_forth(blocks):
    return lax.all_to_all(blocks, "blk", split_axis=0, concat_axis=0, tiled=True)


def column_part(matrix, index, width):
    return lax.dynamic_slice_in_dim(matrix, index * width, width, 1)


def column_sum(values):
    return dot_nn(jnp.ones((8, values.shape[0]), BF), values)[0]


def interleave(matrix):
    rows, columns = matrix.shape
    return matrix.reshape(rows, 2, columns // 256, 128).swapaxes(1, 2).reshape(rows, columns)


def part_again(matrix):
    rows, columns = matrix.shape
    return matrix.reshape(rows, columns // 256, 2, 128).swapaxes(1, 2).reshape(rows, columns)


def pack_small(shifts, gains, bias):
    width = shifts.shape[1]
    rows = jnp.concatenate([shifts, gains, bias.reshape(-1, width)], axis=0)
    return jnp.pad(rows, ((0, 128 - rows.shape[0]), (0, 0)))


def unpack_small(rows, width):
    rows = rows.reshape(-1, 128, width)
    shifts = rows[:, :10].transpose(1, 0, 2).reshape(10, -1)
    gains = rows[:, 10:13].transpose(1, 0, 2).reshape(3, -1)
    return shifts, gains, rows[:, 13:17].reshape(-1)


def per_device(tuned):
    def run(
        decoder_in,
        memory,
        segment_ids,
        memory_lengths,
        w_self_in,
        w_self_out,
        w_cross_query,
        w_cross_pair,
        w_cross_out,
        w_feed_up,
        w_feed_down,
        shifts,
        norm_gains,
        feed_bias,
        out_grad,
    ):
        item_count, length, width = decoder_in.shape
        row_count = item_count * length
        pair_shard = interleave(w_cross_pair)
        blocks = memory.reshape((-1, item_count) + memory.shape[1:])
        sent = [blocks[:, i] for i in range(item_count)]
        half = item_count // 2
        if tuned:
            small = pack_small(shifts, norm_gains, feed_bias)
            first = [small, w_self_in, w_self_out, w_cross_query, pair_shard]
            second = [w_cross_out, w_feed_up, w_feed_down]
            own, own_two = share_of(first, 4, 1), share_of(second, 4)
            across, across_two = swap_x(own), swap_x(own_two)
            across_y, across_two_y = swap_y(across), swap_y(across_two)
            line = along_z(own, (across,))
            own_two = tie(own_two, line, across_y, across_two)
            far, line_y = swap_x(line), swap_y(line)
            line_two = along_z(own_two, (far, across_two_y))
            pair = tie(jnp.stack(sent[:half], axis=1), line_two, line_y)
            pair = back_and_forth(pair)
            arrived = [pair[:, i] for i in range(half)]
            far_two, line_two_y = swap_x(line_two), swap_y(line_two)

            def near(piece, pieces):
                return jnp.concatenate([piece[None], pieces])

            small, self_proj, self_out, cross_query, cross_pair = spread(
                first, [near(across, line), far, near(across_y, line_y), swap_y(far)], 1
            )
            shift_low, gain_low, feed_shift_low = unpack_small(small, shifts.shape[1])
        else:
            def whole(shard, axis=0):
                return lax.all_gather(shard, "blk", axis=axis, tiled=True)

            shift_low, gain_low = whole(shifts, 1), whole(norm_gains, 1)
            feed_shift_low = whole(feed_bias)
            self_proj, self_out, cross_query = whole(w_self_in), whole(w_self_out), whole(w_cross_query)
            cross_pair, cross_out = whole(pair_shard), whole(w_cross_out)
            feed_up, feed_down = whole(w_feed_up), whole(w_feed_down)
            arrived = [back_and_forth(v) for v in sent]
        shift_rows = shift_low.astype(F32)
        gain_rows = gain_low.astype(F32)
        feed_shift = feed_shift_low.astype(F32)
        query_scale = (width // HEADS) ** (-0.5)
        three = (item_count, length, width)

        token_rows = decoder_in.reshape(row_count, width)
        no_shift = jnp.zeros((width,), F32)
        in_shift = jnp.concatenate([shift_rows[0], no_shift, shift_rows[1]])
        in_scale = jnp.concatenate([no_shift + query_scale, no_shift + 1.0, no_shift + 1.0])
        qkv = (
            (jnp.dot(token_rows, self_proj, preferred_element_type=F32) + in_shift) * in_scale
        ).astype(BF).reshape(item_count, length, 3 * width)
        attended, self_logs = self_forward(segment_ids, qkv)
        attended = attended.reshape(row_count, width)
        branch = jnp.dot(attended, self_out, preferred_element_type=F32) + shift_rows[2]
        hidden, first_norm_back = jax.vjp(
            layer_norm, token_rows.astype(F32) + branch, gain_rows[0], shift_rows[7]
        )
        hidden_low = hidden.astype(BF)

        cross_queries = (
            (jnp.dot(hidden_low, cross_query, preferred_element_type=F32) + shift_rows[3])
            * query_scale
        ).astype(BF).reshape(three)
        pair_shift = interleave(jnp.concatenate([no_shift, shift_rows[4]])[None])
        item_lengths = [memory_lengths[i : i + 1] for i in range(item_count)]
        gathered, kvs, outs, cross_logs = None, [], [], []
        if tuned:
            far_two = tie(far_two, cross_queries)
            far_two_y = swap_y(far_two)
        for i in range(item_count):
            if tuned and i == half:
                arrived.append(back_and_forth(tie(sent[i], cross_queries, line_two_y)))
            elif tuned and i > half:
                arrived.append(
                    back_and_forth(tie(sent[i], *arrived[half:], outs[half - 1]))
                )
            source = arrived[i]
            if tuned and i == item_count - 1:
                parts = [near(across_two, line_two), far_two, near(across_two_y, line_two_y), far_two_y]
                cross_out, feed_up, feed_down = spread(
                    second, parts, spots=tie(spot_vector(), outs[i - 1])
                )
                source = tie(source, outs[i - 1], feed_up)
            source = source.reshape(-1, width)
            out, logs, kv, gathered = cross_forward(
                item_lengths[i], cross_queries[i], source, cross_pair, pair_shift,
                i, item_count, gathered,
            )
            kvs.append(kv)
            outs.append(out)
            cross_logs.append(logs)
        cross_attended = jnp.concatenate(outs)
        cross_branch = jnp.dot(cross_attended, cross_out, preferred_element_type=F32) + shift_rows[5]
        second, second_norm_back = jax.vjp(
            layer_norm, hidden + cross_branch, gain_rows[1], shift_rows[8]
        )
        second_low = second.astype(BF)

        upward = jnp.dot(second_low, feed_up, preferred_element_type=F32) + feed_shift
        activation, slope = gelu_and_slope(upward)
        activation_low, slope = activation.astype(BF), slope.astype(BF)
        feed_branch = jnp.dot(activation_low, feed_down, preferred_element_type=F32) + shift_rows[6]
        block_out, third_norm_back = jax.vjp(
            layer_norm, second + feed_branch, gain_rows[2], shift_rows[9]
        )

        third_grad, third_gain, third_shift = third_norm_back(
            out_grad.astype(F32).reshape(row_count, width)
        )
        down_low = third_grad.astype(BF)
        grad_down = dot_tn(activation_low, down_low)
        upward_low, grad_feed_shift, second_grad = feed_backward(down_low, feed_down, slope, feed_up)
        grad_up = dot_tn(second_low, upward_low)
        second_grad = third_grad + second_grad
        cross_grad, second_gain, second_shift = second_norm_back(second_grad)
        cross_low = cross_grad.astype(BF)
        grad_cross_out = dot_tn(cross_attended, cross_low)
        cross_incoming = dot_nt(cross_low, cross_out).astype(BF).reshape(three)
        dqs, value_sums, pair_grad, memory_back = [], 0.0, (), []
        before = None
        for i in range(item_count):
            incoming = cross_incoming[i] if before is None else tie(cross_incoming[i], before)
            if tuned and i == 1:
                lefts = [tie(v, dqs[0]) for v in (activation_low, second_low, cross_attended)]
                sums_one = Reduce(list(zip(lefts, (down_low, upward_low, cross_low))))
            if tuned and i == 2:
                incoming = tie(incoming, *sums_one.over_y(merged=False))
            if i % half == 0:
                back = (blocks.shape[0], half)
            dq, sums, pair_grad, back = cross_backward(
                item_lengths[i], cross_queries[i], incoming, cross_logs[i], kvs[i], cross_pair,
                i, item_count, pair_grad, back,
            )
            before = dq
            if i % half == half - 1:
                memory_back.append(back_and_forth(back))
            value_sums = value_sums + sums[0]
            dqs.append(dq)
        cross_dq = jnp.concatenate(dqs)
        all_sources = gathered.reshape(-1, width)
        all_grads = pair_grad.reshape(-1, 2 * width)
        memory_grad = jnp.concatenate(memory_back, axis=1).reshape(memory.shape)
        cross_query_low = cross_dq * BF(query_scale)
        grad_cross_query = dot_tn(hidden_low, cross_query_low)
        hidden_grad = cross_grad + dot_nt(cross_query_low, cross_query)
        first_grad, first_gain, first_shift = first_norm_back(hidden_grad)
        self_low = first_grad.astype(BF)
        grad_self_out = dot_tn(attended, self_low)
        self_incoming = dot_nt(self_low, self_out).astype(BF).reshape(three)
        if tuned:
            grad_pair = dot_tn(all_sources, all_grads).astype(BF)
            sums_two = Reduce([(hidden_low, cross_query_low), tie(grad_pair, memory_back[0])])
            self_incoming = tie(self_incoming, sums_one.over_x(), *sums_two.sent)
        joined_grad = self_backward(segment_ids, qkv, self_incoming, self_logs)
        joined_grad = joined_grad.reshape(row_count, 3 * width)
        if tuned:
            joined_grad = tie(joined_grad, *sums_two.over_y())
        grad_self = dot_tn(token_rows, joined_grad)
        decoder_grad = (
            (first_grad + dot_nt(joined_grad, self_proj)).astype(BF).reshape(decoder_in.shape)
        )
        joined_sums = column_sum(joined_grad)
        grad_shift_rows = jnp.stack(
            [
                joined_sums[:width],
                joined_sums[2 * width :],
                column_sum(self_low),
                column_sum(cross_query_low),
                value_sums,
                column_sum(cross_low),
                column_sum(down_low),
                first_shift,
                second_shift,
                third_shift,
            ]
        )
        grad_gain_rows = jnp.stack([first_gain, second_gain, third_gain])
        grad_feed_shift = grad_feed_shift[0]
        block_low = block_out.astype(BF).reshape(decoder_in.shape)
        if tuned:
            count = shifts.shape[1]
            packed = jnp.concatenate(
                [
                    grad_shift_rows.reshape(10, 8, count),
                    grad_gain_rows.reshape(3, 8, count),
                    grad_feed_shift.reshape(8, -1, count).swapaxes(0, 1),
                ],
                axis=0,
            ).swapaxes(0, 1)
            packed = jnp.pad(packed, ((0, 0), (0, 128 - packed.shape[1]), (0, 7 * count)))
            sums_three = Reduce(
                [
                    (attended, self_low),
                    (token_rows, joined_grad),
                    packed.reshape(-1, 8 * count).astype(BF),
                ]
            )
            sums_three.over_y()
            sums_two.over_x()
            sums_three.over_x(memory_back[1])
            sums_one.over_z((), (sums_two.got,), (sums_three.got,))
            sums_three.join(sums_two)
            sums_three.over_z()
            down, up, out = sums_one.share()
            own_out, own_in, sums, query, pair = sums_three.share()
            shift_share, gain_share = sums[:10, :count], sums[10:13, :count]
            feed_share = sums[13:17, :count].reshape(-1)
        else:
            grad_pair = dot_tn(all_sources, all_grads)

            def share(value, dim=0):
                part = lax.psum_scatter(value, "blk", scatter_dimension=dim, tiled=True)
                return lax.psum(part.astype(BF), "items").astype(F32)

            large = [grad_down, grad_up, grad_cross_out, grad_cross_query, grad_pair, grad_self_out, grad_self]
            down, up, out, query, pair, own_out, own_in = [share(grad) for grad in large]
            shift_share, gain_share = share(grad_shift_rows, 1), share(grad_gain_rows, 1)
            feed_share = share(grad_feed_shift)
        return (
            block_low,
            decoder_grad,
            memory_grad,
            own_in,
            own_out,
            query,
            part_again(pair),
            out,
            up,
            down,
            shift_share,
            gain_share,
            feed_share,
        )

    return run


def solution(mesh):
    in_specs = (
        P(("items", "blk"), None, None),
        P("items", "blk", None),
        P(("items", "blk"), None),
        P(("items", "blk")),
        P("blk", None),
        P("blk", None),
        P("blk", None),
        P("blk", None),
        P("blk", None),
        P("blk", None),
        P("blk", None),
        P(None, "blk"),
        P(None, "blk"),
        P("blk"),
        P(("items", "blk"), None, None),
    )
    out_specs = (
        P(("items", "blk"), None, None),
        P(("items", "blk"), None, None),
        P("items", "blk", None),
        P("blk", None),
        P("blk", None),
        P("blk", None),
        P("blk", None),
        P("blk", None),
        P("blk", None),
        P("blk", None),
        P(None, "blk"),
        P(None, "blk"),
        P("blk"),
    )
    tuned = mesh.shape["blk"] == 8 and mesh.shape["items"] == 4
    return jax.shard_map(
        per_device(tuned), mesh=mesh, in_specs=in_specs, out_specs=out_specs, check_vma=False
    )
```
